512 devices in a mesh: grp: 16 (over y, x_lo, core), blk: 32 (over x_hi, z).
Axes of the slice: x: 4 (x_hi: 2, x_lo: 2; x = x_hi * 2 + x_lo), y: 4, z: 16, core: 2. Of those that a mesh axis runs over, the one named last changes fastest.
Arguments:
- src_emb: float32 [400, 65536], P(None, ('grp', 'blk')), may hold values from -1.5 to 1.5
- src_state: float32 [65536], P(('grp', 'blk')), may hold values from 0.01 to 1
- dst_emb: float32 [400, 65536], P(None, ('grp', 'blk')), may hold values from -1.5 to 1.5
- dst_state: float32 [65536], P(('grp', 'blk')), may hold values from 0.01 to 1
- relations: float32 [8, 400], replicated, may hold values from 0.1 to 1.9
- rel_state: float32 [8], replicated, may hold values from 100 to 10000
- src_ids: int32 [4096, 128], P(('grp', 'blk')), may hold values from 0 to 127
- dst_ids: int32 [4096, 128], P(('grp', 'blk')), may hold values from 0 to 127
- rel_ids: int32 [4096, 128], P(('grp', 'blk')), may hold values from 0 to 7
- neg_ids: int32 [4096, 64], P(('grp', 'blk')), may hold values from 0 to 127
- lengths: int32 [4096], P(('grp', 'blk')), may hold values from 16 to 128, as said below
Outputs:
- src_out: float32 [400, 65536], P(None, ('grp', 'blk'))
- src_state_out: float32 [65536], P(('grp', 'blk'))
- dst_out: float32 [400, 65536], P(None, ('grp', 'blk'))
- dst_state_out: float32 [65536], P(('grp', 'blk'))
- relations_out: float32 [8, 400], replicated
The draws below stay inside these ranges and needn't reach their ends.
Inputs may be any that keep to these rules, and one draw needn't show every extreme that they name: `lengths`: slots at or beyond a bucket's length are padding; some bucket of every draw is full, and each length is at least 16.
All inputs are finite; a program needn't handle non-finite values.
Results may differ from the reference program's by a relative error of at most 0.0003.
Values sent between devices are 32-bit elements; how exact they have to be, the bound alone decides.
A program may use at most 64 MiB of HBM per device.

```python
import math
import jax
import jax.numpy as jnp
from jax import lax

D = 400
NREL = 8
ROWS = 128
BATCH = 128
NEG = 64
ROUNDS = 8
NODES = 65536
BUCKETS = 4096
N_GRP = 16
N_BLK = 32


def draw_lengths(key, part):
    key = jax.random.fold_in(key, 11)
    first, second = jax.random.split(key)
    count = N_GRP * N_BLK * ROUNDS
    lowest = max(1, BATCH // 8)
    values = jax.random.randint(first, (count,), lowest, BATCH + 1)
    where = jax.random.randint(second, (), 0, count)
    return values.at[where].set(BATCH).astype(jnp.int32)


def touch_ends(drawn, own_key, smallest, top_value):
    extent = drawn.shape
    index_at = [jax.random.randint(jax.random.fold_in(own_key, axis), (), 0, extent[axis]) for axis in range(len(extent))]
    drawn = drawn.at[tuple(index_at)].set(smallest)
    longest = extent.index(max(extent))
    index_at[longest] = (index_at[longest] + 1) % extent[longest]
    return drawn.at[tuple(index_at)].set(top_value)


def shard_levels(rng, shape, cuts, smallest, high):
    factor_of, own = 1.0, jax.random.fold_in(rng, 6)
    for position, blocks in cuts:
        steps = jnp.exp(jax.random.uniform(jax.random.fold_in(own, position), (blocks,), jnp.float32, smallest / len(cuts), high / len(cuts)))
        factor_of = factor_of * jnp.repeat(steps, shape[position] // blocks).reshape([-1 if axis == position else 1 for axis in range(len(shape))])
    return factor_of


def centred(stream_key, dims, deviation, limit, shards=(), kind=jnp.bfloat16):
    drawn = jax.random.normal(stream_key, dims, jnp.float32) * deviation
    if len(shards) > 0:
        drawn = shard_levels(stream_key, dims, shards, -0.22, 0.18) * drawn
    return jnp.clip(drawn, min=-limit, max=limit).astype(kind)


def setup_inputs(seed: int = 0) -> dict:
    seeds = jax.random.split(jax.random.key(seed), 12)
    src_emb = centred(seeds[0], (D, NODES), 0.22, 1.5, ((1, 512),), jnp.float32)
    src_state = jnp.clip(jnp.exp(math.log(1.0) - 4.6051702 * jax.random.uniform(seeds[1], (NODES,), jnp.float32) ** shard_levels(seeds[1], (NODES,), ((0, 512),), -0.2, 0.2)), 0.01, 1.0)
    dst_emb = centred(seeds[2], (D, NODES), 0.22, 1.5, ((1, 512),), jnp.float32)
    dst_state = jnp.clip(jnp.exp(math.log(1.0) - 4.6051702 * jax.random.uniform(seeds[3], (NODES,), jnp.float32) ** shard_levels(seeds[3], (NODES,), ((0, 512),), -0.2, 0.2)), 0.01, 1.0)
    relations = jnp.clip(1.0 + 0.18 * jax.random.normal(seeds[4], (NREL, D), jnp.float32), 0.1, 1.9)
    rel_state = jnp.clip(jnp.exp(jax.random.uniform(seeds[5], (NREL,), jnp.float32, math.log(100.0), math.log(10000.0))), 100.0, 10000.0)
    src_ids = touch_ends(jax.random.randint(seeds[6], (BUCKETS, BATCH), 0, ROWS), jax.random.fold_in(seeds[6], 1), 0, ROWS - 1).astype(jnp.int32)
    dst_ids = touch_ends(jax.random.randint(seeds[7], (BUCKETS, BATCH), 0, ROWS), jax.random.fold_in(seeds[7], 1), 0, ROWS - 1).astype(jnp.int32)
    rel_ids = touch_ends(jax.random.randint(seeds[8], (BUCKETS, BATCH), 0, NREL), jax.random.fold_in(seeds[8], 1), 0, NREL - 1).astype(jnp.int32)
    neg_ids = touch_ends(jax.random.randint(seeds[9], (BUCKETS, NEG), 0, ROWS), jax.random.fold_in(seeds[9], 1), 0, ROWS - 1).astype(jnp.int32)
    lengths = draw_lengths(jax.random.fold_in(seeds[11], 71), 0)
    return dict(src_emb=src_emb, src_state=src_state, dst_emb=dst_emb, dst_state=dst_state, relations=relations, rel_state=rel_state, src_ids=src_ids, dst_ids=dst_ids, rel_ids=rel_ids, neg_ids=neg_ids, lengths=lengths)


learn_rate = 0.1
rel_rate = 0.5
epsilon = 1e-08

def bucket_grads(src_rows, dst_rows, neg_rows, w_rows, valid_mask):
    highest = lax.Precision.HIGHEST
    weighted = src_rows * w_rows
    positive = lax.optimization_barrier(jnp.sum(weighted * dst_rows, axis=0))
    negative = jnp.einsum('kb,kn->bn', weighted, neg_rows, precision=highest)
    g_pos = -jax.nn.sigmoid(-positive) * valid_mask
    g_neg = jax.nn.sigmoid(negative) * valid_mask[:, None]
    combined = g_pos[None, :] * dst_rows + jnp.einsum('bn,kn->kb', g_neg, neg_rows, precision=highest)
    g_dst = g_pos[None, :] * weighted
    g_negrows = jnp.einsum('bn,kb->kn', g_neg, weighted, precision=highest)
    return (w_rows * combined, src_rows * combined, jnp.concatenate([g_dst, g_negrows], axis=1))

def apply_rows(emb_block, row_state, slot_ids, grads):
    summed = jnp.zeros_like(emb_block).at[:, slot_ids].add(grads)
    row_state = row_state + lax.optimization_barrier(jnp.mean(summed * summed, axis=0))
    emb_block = emb_block - learn_rate * summed / (jnp.sqrt(row_state)[None, :] + epsilon)
    return (emb_block, row_state)

def train_bucket(src_blk, src_st, dst_blk, dst_st, relations, s_ids, d_ids, r_ids, n_ids, valid_count):
    batch = s_ids.shape[0]
    valid_mask = (jnp.arange(batch, dtype=jnp.int32) < valid_count).astype(jnp.float32)
    src_rows = jnp.take(src_blk, s_ids, axis=1)
    slot_ids = jnp.concatenate([d_ids, n_ids]).astype(jnp.int32)
    slot_rows = jnp.take(dst_blk, slot_ids, axis=1)
    w_rows = jnp.take(relations, r_ids, axis=0).T
    g_src, g_rel, g_slots = bucket_grads(src_rows, slot_rows[:, :batch], slot_rows[:, batch:], w_rows, valid_mask)
    one_hot = (r_ids[:, None] == jnp.arange(relations.shape[0], dtype=jnp.int32)[None, :]).astype(jnp.float32)
    rel_grad = jnp.einsum('br,kb->rk', one_hot, g_rel, precision=lax.Precision.HIGHEST)
    src_blk, src_st = apply_rows(src_blk, src_st, s_ids, g_src)
    dst_blk, dst_st = apply_rows(dst_blk, dst_st, slot_ids, g_slots)
    return (src_blk, src_st, dst_blk, dst_st, rel_grad)

def reference(src_emb, src_state, dst_emb, dst_state, relations, rel_state, src_ids, dst_ids, rel_ids, neg_ids, lengths):
    groups, blocks = (N_GRP, N_BLK)
    src_blocks = src_emb.reshape(D, groups, blocks, ROWS).transpose(1, 2, 0, 3)
    dst_blocks = dst_emb.reshape(D, groups, blocks, ROWS).transpose(1, 2, 0, 3)
    src_st = src_state.reshape(groups, blocks, ROWS)
    dst_st = dst_state.reshape(groups, blocks, ROWS)
    s_all = src_ids.reshape(groups, blocks, ROUNDS, BATCH)
    d_all = dst_ids.reshape(groups, blocks, ROUNDS, BATCH)
    r_all = rel_ids.reshape(groups, blocks, ROUNDS, BATCH)
    n_all = neg_ids.reshape(groups, blocks, ROUNDS, NEG)
    l_all = lengths.reshape(groups, blocks, ROUNDS)
    inner = jax.vmap(train_bucket, in_axes=(0, 0, 0, 0, None, 0, 0, 0, 0, 0))
    rel_total = jnp.zeros((NREL, D), jnp.float32)
    for round_index in range(ROUNDS):
        cur_dst = jnp.roll(dst_blocks, round_index, axis=1)
        cur_st = jnp.roll(dst_st, round_index, axis=1)

        def per_group(items):
            return inner(items[0], items[1], items[2], items[3], relations, items[4], items[5], items[6], items[7], items[8])
        outcome = lax.map(per_group, (src_blocks, src_st, cur_dst, cur_st, s_all[:, :, round_index], d_all[:, :, round_index], r_all[:, :, round_index], n_all[:, :, round_index], l_all[:, :, round_index]))
        src_blocks, src_st = (outcome[0], outcome[1])
        dst_blocks = jnp.roll(outcome[2], -round_index, axis=1)
        dst_st = jnp.roll(outcome[3], -round_index, axis=1)
        rel_total = rel_total + lax.optimization_barrier(jnp.sum(outcome[4], axis=(0, 1)))
    rstate = rel_state + lax.optimization_barrier(jnp.mean(rel_total * rel_total, axis=1))
    relations_out = relations - rel_rate * rel_total / (jnp.sqrt(rstate)[:, None] + epsilon)
    src_out = src_blocks.transpose(2, 0, 1, 3).reshape(D, -1)
    dst_out = dst_blocks.transpose(2, 0, 1, 3).reshape(D, -1)
    return (src_out, src_st.reshape(-1), dst_out, dst_st.reshape(-1), relations_out)
```

```python
import jax
import jax.numpy as jnp
from jax import lax
from jax.experimental import pallas as pl
from jax.experimental.pallas import tpu as pltpu
from jax.sharding import PartitionSpec as P

learn_rate = 0.1
rel_rate = 0.5
epsilon = 1e-08

D = 400
NREL = 8
ROWS = 128
NEG = 64
ROUNDS = 8
N_GRP = 16
N_BLK = 32
Z = 16

CHUNKS = ((0, 128), (128, 128), (256, 144))
NC = len(CHUNKS)
STATE = D
MOVED = D + 8
MESH = pl.DeviceIdType.MESH
f32, bf16 = jnp.float32, jnp.bfloat16


def halves(x):
    hi = x.astype(bf16)
    return hi, (x - hi.astype(f32)).astype(bf16)


def nn(a, b):
    return lax.dot_general(a, b, (((1,), (0,)), ((), ())), preferred_element_type=f32)


def nt(a, b):
    return lax.dot_general(a, b, (((1,), (1,)), ((), ())), preferred_element_type=f32)


def folded(x):
    return x[:, :ROWS] + x[:, ROWS:]


def picked(table, row):
    index = jnp.broadcast_to(row, table.shape)
    return jnp.take_along_axis(table, index, axis=1, mode="promise_in_bounds")


def sub_iota():
    return lax.broadcasted_iota(jnp.int32, (ROWS, ROWS), 0)


def window(
    lengths,
    rel_state,
    src_e,
    src_s,
    dst_e,
    dst_s,
    rel,
    s_ids,
    d_ids,
    r_ids,
    n_ids,
    src_o,
    src_so,
    dst_o,
    dst_so,
    rel_o,
    mov,
    back,
    w_buf,
    s_buf,
    fixed_t,
    a2,
    d2,
    rel_t,
    rg,
    c1,
    dv,
    packed,
    gotten,
    tiles,
    r1,
    r2,
    r3,
    r4,
    r5,
    send_sem,
    recv_sem,
    back_sem,
    id_send,
    id_recv,
    ar_send,
    ar_recv,
):
    g, b = lax.axis_index("grp"), lax.axis_index("blk")
    y, x_lo, core = g // 4, (g // 2) % 2, g % 2
    x_hi, z = b // Z, b % Z

    def blk(by):
        return (b + by + N_BLK) % N_BLK

    def y_peer(i):
        q = (y + i) % 4
        return q, (q * 4 + x_lo * 2 + core, b)

    def xc_peer(i):
        q = (x_hi * 4 + x_lo * 2 + core + i) % 8
        return q, (y * 4 + q % 4, (q // 4) * Z + z)

    def zl_peer(i):
        q = (z % 4 + i) % 4
        return q, (g, x_hi * Z + (z // 4) * 4 + q)

    def zh_peer(i):
        q = (z // 4 + i) % 4
        return q, (g, x_hi * Z + q * 4 + z % 4)

    stages = ((y_peer, 4), (xc_peer, 8), (zl_peer, 4), (zh_peer, 4))

    barrier = pltpu.get_barrier_semaphore()

    def greet(device):
        pl.semaphore_signal(barrier, inc=1, device_id=device, device_id_type=MESH)

    for peer, n in stages:
        for i in range(1, n):
            greet(peer(i)[1])
    n_peers = sum(n - 1 for _, n in stages)

    for k in range(ROUNDS):
        packed[k, 0:1, :] = s_ids[k : k + 1, :]
        packed[k, 1:2, :] = d_ids[k : k + 1, :]
        packed[k, 2:3, :] = r_ids[k : k + 1, :]
        packed[k, 3:4, :] = jnp.concatenate([n_ids[k : k + 1, :], jnp.full((1, ROWS - NEG), -1, jnp.int32)], axis=1)
        packed[k, 4:8, :] = jnp.full((4, ROWS), lengths[k], jnp.int32)

    wide = jnp.concatenate([rel[...], jnp.zeros((NREL, 512 - D), f32)], axis=1)
    wide = jnp.concatenate([wide, jnp.zeros((ROWS - NREL, 512), f32)], axis=0)
    rel_t[...] = wide.T[:D, :]
    rg[...] = jnp.zeros_like(rg)

    def moved_copy(k, c, device):
        rows = pl.ds(CHUNKS[c][0], CHUNKS[c][1] + (8 if c == NC - 1 else 0))
        return pltpu.make_async_remote_copy(
            src_ref=mov.at[k, rows],
            dst_ref=mov.at[jnp.minimum(k + 1, ROUNDS - 1), rows],
            send_sem=send_sem.at[k, c],
            recv_sem=recv_sem.at[jnp.minimum(k + 1, ROUNDS - 1), c],
            device_id=device,
            device_id_type=MESH,
        )

    def arrived(k, c):
        rows = pl.ds(CHUNKS[c][0], CHUNKS[c][1] + (8 if c == NC - 1 else 0))
        pltpu.make_async_remote_copy(
            src_ref=mov.at[k, rows],
            dst_ref=mov.at[k, rows],
            send_sem=send_sem.at[k, c],
            recv_sem=recv_sem.at[k, c],
            device_id=(g, blk(1)),
            device_id_type=MESH,
        ).wait_recv()

    def home_copy(c, out, device):
        rows = pl.ds(*CHUNKS[c])
        return pltpu.make_async_remote_copy(
            src_ref=mov.at[ROUNDS - 1, rows],
            dst_ref=out.at[rows],
            send_sem=send_sem.at[ROUNDS - 1, c],
            recv_sem=back_sem.at[c],
            device_id=device,
            device_id_type=MESH,
        )

    def home_state_copy(device):
        return pltpu.make_async_remote_copy(
            src_ref=mov.at[ROUNDS - 1, pl.ds(STATE, 8)],
            dst_ref=back,
            send_sem=send_sem.at[ROUNDS - 1, NC],
            recv_sem=back_sem.at[NC],
            device_id=device,
            device_id_type=MESH,
        )

    def stepped(k, grad, out, next_device, home_device):
        state = mov[k, STATE : STATE + 8, :] + jnp.sum(grad * grad, axis=0, keepdims=True) * (1.0 / D)
        scale = (learn_rate / (jnp.sqrt(state) + epsilon))[0:1]
        mov[k, STATE : STATE + 8, :] = state
        for c, (r0, n) in enumerate(CHUNKS):
            mov[k, r0 : r0 + n, :] = mov[k, r0 : r0 + n, :] - grad[r0 : r0 + n] * scale

            @pl.when(k < ROUNDS - 1)
            def _():
                moved_copy(k, c, next_device).start()

            @pl.when(k == ROUNDS - 1)
            def _():
                home_copy(c, out, home_device).start()
                if c == NC - 1:
                    home_state_copy(home_device).start()

    def settled(table, state, grad):
        new = state[...] + jnp.sum(grad * grad, axis=0, keepdims=True) * (1.0 / D)
        state[...] = new
        table[...] = table[...] - grad * (learn_rate / (jnp.sqrt(new) + epsilon))

    def coefficients(tile):
        rows = sub_iota()
        valid = (lax.broadcasted_iota(jnp.int32, (1, ROWS), 1) < tile[4:5]).astype(f32)
        hit = (rows == tile[1:2]).astype(f32)
        count = jnp.sum((rows == tile[3:4]).astype(f32), axis=1, keepdims=True)
        return (count + hit) * valid, hit * valid

    def one_hot2(row):
        hot = (sub_iota() == row).astype(f32).astype(bf16)
        return jnp.concatenate([hot, hot], axis=1)

    def quadrants(x):
        return (x[:ROWS, :ROWS] + x[ROWS:, ROWS:]) + (x[:ROWS, ROWS:] + x[ROWS:, :ROWS])

    def two_by_two(hi, lo):
        line = jnp.concatenate([hi, lo], axis=1)
        return jnp.concatenate([line, line], axis=0)

    def two_by_two_t(hi, lo):
        return jnp.concatenate([jnp.concatenate([hi, hi], axis=1), jnp.concatenate([lo, lo], axis=1)], axis=0)

    def split_into(ref, r0, n, x):
        hi, lo = halves(x)
        ref[r0 : r0 + n, :ROWS] = hi
        ref[r0 : r0 + n, ROWS:] = lo

    def transposed_into(x):
        hi, lo = halves(x.T)
        fixed_t[:ROWS, :] = hi
        fixed_t[ROWS:, :] = lo

    def both(x):
        return jnp.concatenate(halves(x), axis=1)

    @pl.when(core == 0)
    def _():
        greet((g, blk(-1)))
        greet((g, blk(ROUNDS - 1)))
        src_o[...] = src_e[...]
        src_so[...] = src_s[...]
        mov[0, :D, :] = dst_e[...]
        mov[0, STATE : STATE + 8, :] = jnp.broadcast_to(dst_s[...], (8, ROWS))

        def prepare(k):
            tile = packed[k]
            w = picked(rel_t[...], tile[2:3])
            s = picked(src_o[...], tile[0:1])
            a = s * w
            w_buf[...] = w
            s_buf[...] = s
            split_into(a2, 0, D, a)
            transposed_into(a)
            c, v = coefficients(tile)
            c1[...] = c.T
            dv[...] = v.T

        prepare(0)
        pl.semaphore_wait(barrier, n_peers + 2)

        @pl.loop(0, ROUNDS)
        def _(k):
            total = jnp.zeros((2 * ROWS, 2 * ROWS), f32)
            for c, (r0, n) in enumerate(CHUNKS):

                @pl.when(k > 0)
                def _():
                    arrived(k, c)

                split_into(d2, r0, n, mov[k, r0 : r0 + n, :])
                total = total + nn(fixed_t[:, r0 : r0 + n], d2[r0 : r0 + n, :])
            m = c1[...] * jax.nn.sigmoid(quadrants(total)) - dv[...]
            hi, lo = halves(m)
            stepped(k, folded(nn(a2[...], two_by_two(hi, lo))), dst_o, (g, blk(1)), (g, blk(1 - ROUNDS)))

            h = folded(nt(d2[...], two_by_two_t(hi, lo)))
            tile = packed[k]
            settled(src_o, src_so, nt(both(w_buf[...] * h), one_hot2(tile[0:1])))
            rg[:D, :] = rg[:D, :] + nt(both(s_buf[...] * h), one_hot2(tile[2:3]))

            @pl.when(k < ROUNDS - 1)
            def _():
                prepare(k + 1)

    @pl.when(core == 1)
    def _():
        for k in range(1, ROUNDS):
            greet((g, blk(k)))
        greet((g, blk(1 - ROUNDS)))
        dst_o[...] = dst_e[...]
        dst_so[...] = dst_s[...]
        mov[0, :D, :] = src_e[...]
        mov[0, STATE : STATE + 8, :] = jnp.broadcast_to(src_s[...], (8, ROWS))
        gotten[0] = packed[0]

        def id_copy(k):
            return pltpu.make_async_remote_copy(
                src_ref=packed.at[k],
                dst_ref=gotten.at[k],
                send_sem=id_send.at[k],
                recv_sem=id_recv.at[k],
                device_id=(g, blk(-k)),
                device_id_type=MESH,
            )

        def prepare(k):
            tile = gotten[k]
            w_buf[...] = picked(rel_t[...], tile[2:3])
            d = dst_o[...]
            split_into(d2, 0, D, d)
            transposed_into(d)
            c, v = coefficients(tile)
            c1[...] = c
            dv[...] = v

        prepare(0)
        pl.semaphore_wait(barrier, n_peers + ROUNDS)
        for k in range(1, ROUNDS):
            id_copy(k).start()

        @pl.loop(0, ROUNDS)
        def _(k):
            tile = gotten[k]
            total = jnp.zeros((2 * ROWS, 2 * ROWS), f32)
            for c, (r0, n) in enumerate(CHUNKS):

                @pl.when(k > 0)
                def _():
                    arrived(k, c)

                s = picked(mov[k, r0 : r0 + n, :], tile[0:1])
                s_buf[r0 : r0 + n, :] = s
                split_into(a2, r0, n, s * w_buf[r0 : r0 + n, :])
                total = total + nn(fixed_t[:, r0 : r0 + n], a2[r0 : r0 + n, :])
            m = c1[...] * jax.nn.sigmoid(quadrants(total)) - dv[...]
            hi, lo = halves(m)
            h = folded(nn(d2[...], two_by_two(hi, lo)))
            grad = nt(both(w_buf[...] * h), one_hot2(tile[0:1]))
            stepped(k, grad, src_o, (g, blk(-1)), (g, blk(ROUNDS - 1)))

            rg[:D, :] = rg[:D, :] + nt(both(s_buf[...] * h), one_hot2(tile[2:3]))
            settled(dst_o, dst_so, folded(nt(a2[...], two_by_two_t(hi, lo))))

            @pl.when(k < ROUNDS - 1)
            def _():
                id_copy(k + 1).wait_recv()
                prepare(k + 1)

        for k in range(1, ROUNDS):
            id_copy(k).wait_send()

    summed = rg[...].T[:NREL, :]
    for q in range(4):
        tiles[q] = summed[:, q * ROWS : (q + 1) * ROWS]

    first = 0

    def exchange(stage, peer, n, source, buf):
        def copy(i, slot):
            q, device = peer(i)
            return pltpu.make_async_remote_copy(
                src_ref=source(q),
                dst_ref=buf.at[slot],
                send_sem=ar_send.at[stage, q],
                recv_sem=ar_recv.at[stage, slot],
                device_id=device,
                device_id_type=MESH,
            )

        mine = peer(0)[0]
        for i in range(1, n):
            copy(i, mine).start()
        for i in range(1, n):
            copy(i, peer(i)[0]).wait_recv()
        return lambda: [copy(i, mine).wait_send() for i in range(1, n)]

    def added(buf, n):
        value = buf[0]
        for q in range(1, n):
            value = value + buf[q]
        return value

    r1[y] = tiles[y]
    ends = [exchange(0, y_peer, 4, lambda q: tiles.at[q], r1)]
    value = added(r1, 4)
    for stage, (peer, n), buf in ((1, stages[1], r2), (2, stages[2], r3), (3, stages[3], r4)):
        mine = peer(0)[0]
        buf[mine] = value
        ends.append(exchange(stage, peer, n, lambda q, buf=buf, mine=mine: buf.at[mine], buf))
        value = added(buf, n)
    r5[y] = value
    ends.append(exchange(4, y_peer, 4, lambda q: r5.at[y], r5))

    square = r5[0] * r5[0]
    for q in range(1, 4):
        square = square + r5[q] * r5[q]
    old = jnp.zeros((NREL, 1), f32)
    which = lax.broadcasted_iota(jnp.int32, (NREL, 1), 0)
    for r in range(NREL):
        old = jnp.where(which == r, rel_state[r], old)
    rstate = old + jnp.sum(square, axis=1, keepdims=True) * (1.0 / D)
    scale = rel_rate / (jnp.sqrt(rstate) + epsilon)
    for q in range(4):
        lo, hi = q * ROWS, min(D, (q + 1) * ROWS)
        rel_o[:, lo:hi] = rel[:, lo:hi] - r5[q][:, : hi - lo] * scale

    for end in ends:
        end()

    @pl.loop(0, ROUNDS - 1)
    def _(k):
        for c in range(NC):
            moved_copy(k, c, (g, blk(1))).wait_send()

    def closed(out, state_out):
        for c in range(NC):
            home_copy(c, out, (g, blk(1))).wait_recv()
            home_copy(c, out, (g, blk(1))).wait_send()
        home_state_copy((g, blk(1))).wait_recv()
        home_state_copy((g, blk(1))).wait_send()
        state_out[...] = back[0:1, :]

    @pl.when(core == 0)
    def _():
        closed(dst_o, dst_so)

    @pl.when(core == 1)
    def _():
        closed(src_o, src_so)


def local(src_emb, src_state, dst_emb, dst_state, relations, rel_state, src_ids, dst_ids, rel_ids, neg_ids, lengths):
    vmem, smem = pl.BlockSpec(memory_space=pltpu.VMEM), pl.BlockSpec(memory_space=pltpu.SMEM)
    table, line = jax.ShapeDtypeStruct((D, ROWS), f32), jax.ShapeDtypeStruct((1, ROWS), f32)
    outs = pl.pallas_call(
        window,
        out_shape=[table, line, table, line, jax.ShapeDtypeStruct((NREL, D), f32)],
        in_specs=[smem, smem] + [vmem] * 9,
        out_specs=[vmem] * 5,
        scratch_shapes=[
            pltpu.VMEM((ROUNDS, MOVED, ROWS), f32),
            pltpu.VMEM((8, ROWS), f32),
            pltpu.VMEM((D, ROWS), f32),
            pltpu.VMEM((D, ROWS), f32),
            pltpu.VMEM((2 * ROWS, D), bf16),
            pltpu.VMEM((D, 2 * ROWS), bf16),
            pltpu.VMEM((D, 2 * ROWS), bf16),
            pltpu.VMEM((D, ROWS), f32),
            pltpu.VMEM((512, ROWS), f32),
            pltpu.VMEM((ROWS, ROWS), f32),
            pltpu.VMEM((ROWS, ROWS), f32),
            pltpu.VMEM((ROUNDS, 8, ROWS), jnp.int32),
            pltpu.VMEM((ROUNDS, 8, ROWS), jnp.int32),
            pltpu.VMEM((4, 8, ROWS), f32),
            pltpu.VMEM((4, 8, ROWS), f32),
            pltpu.VMEM((8, 8, ROWS), f32),
            pltpu.VMEM((4, 8, ROWS), f32),
            pltpu.VMEM((4, 8, ROWS), f32),
            pltpu.VMEM((4, 8, ROWS), f32),
            pltpu.SemaphoreType.DMA((ROUNDS, NC + 1)),
            pltpu.SemaphoreType.DMA((ROUNDS, NC)),
            pltpu.SemaphoreType.DMA((NC + 1,)),
            pltpu.SemaphoreType.DMA((ROUNDS,)),
            pltpu.SemaphoreType.DMA((ROUNDS,)),
            pltpu.SemaphoreType.DMA((5, 8)),
            pltpu.SemaphoreType.DMA((5, 8)),
        ],
        compiler_params=pltpu.CompilerParams(
            collective_id=0, has_side_effects=True, vmem_limit_bytes=24 * 1024 * 1024
        ),
    )(
        lengths,
        rel_state,
        src_emb,
        src_state.reshape(1, ROWS),
        dst_emb,
        dst_state.reshape(1, ROWS),
        relations,
        src_ids,
        dst_ids,
        rel_ids,
        neg_ids,
    )
    return (outs[0], outs[1].reshape(ROWS), outs[2], outs[3].reshape(ROWS), outs[4])


def solution(mesh):
    both = ("grp", "blk")
    placed = (
        P(None, both),
        P(both),
        P(None, both),
        P(both),
        P(),
        P(),
        P(both, None),
        P(both, None),
        P(both, None),
        P(both, None),
        P(both),
    )
    return jax.shard_map(
        local,
        mesh=mesh,
        in_specs=placed,
        out_specs=(P(None, both), P(both), P(None, both), P(both), P()),
        check_vma=False,
    )
```

```python
import jax
import jax.numpy as jnp
from jax import lax
from jax.experimental import pallas as pl
from jax.experimental.pallas import tpu as pltpu
from jax.sharding import PartitionSpec as P

learn_rate = 0.1
rel_rate = 0.5
epsilon = 1e-08

D = 400
NREL = 8
ROWS = 128
NEG = 64
ROUNDS = 8
N_GRP = 16
N_BLK = 32
Z = 16

CHUNKS = ((0, 128), (128, 128), (256, 144))
NC = len(CHUNKS)
HOME = ((0, 200), (200, 200))
NH = len(HOME)
PART1, PART2, PART3 = (NH,), (0,), (1,)
STATE = D
MOVED = D + 8
MESH = pl.DeviceIdType.MESH
f32, bf16 = jnp.float32, jnp.bfloat16


def halves(x):
    hi = x.astype(bf16)
    return hi, (x - hi.astype(f32)).astype(bf16)


def nn(a, b):
    return lax.dot_general(a, b, (((1,), (0,)), ((), ())), preferred_element_type=f32)


def nt(a, b):
    return lax.dot_general(a, b, (((1,), (1,)), ((), ())), preferred_element_type=f32)


def folded(x):
    return x[:, :ROWS] + x[:, ROWS:]


def picked(table, row):
    index = jnp.broadcast_to(row, table.shape)
    return jnp.take_along_axis(table, index, axis=1, mode="promise_in_bounds")


def sub_iota():
    return lax.broadcasted_iota(jnp.int32, (ROWS, ROWS), 0)


def window(
    lengths_h,
    rel_state_h,
    src_e,
    src_s,
    dst_e,
    dst_s,
    rel_h,
    s_ids_h,
    d_ids_h,
    r_ids_h,
    n_ids_h,
    stay,
    stay_st,
    home,
    home_st,
    rel_o,
    lengths,
    rel_state,
    rel,
    s_ids,
    d_ids,
    r_ids,
    n_ids,
    line,
    mov,
    w_buf,
    s_buf,
    fixed_t,
    a2,
    d2,
    rel_t,
    rg,
    c1,
    dv,
    packed,
    gotten,
    tiles,
    r1,
    r2,
    r3,
    in_sem,
    send_sem,
    recv_sem,
    back_sem,
    id_send,
    id_recv,
    ar_send,
    ar_recv,
):
    g, b = lax.axis_index("grp"), lax.axis_index("blk")
    y, xc, core = g // 4, (b // Z) * 4 + g % 4, g % 2
    x_hi, z = b // Z, b % Z

    small = [
        pltpu.make_async_copy(a, into, in_sem.at[i])
        for i, (a, into) in enumerate(
            (
                (r_ids_h, r_ids),
                (s_ids_h, s_ids),
                (rel_h, rel),
                (d_ids_h, d_ids),
                (n_ids_h, n_ids),
                (lengths_h, lengths),
                (rel_state_h, rel_state),
            )
        )
    ]
    n_small = len(small)

    def tables(keep, keep_st, move, move_st):
        return [
            pltpu.make_async_copy(a, into, in_sem.at[n_small + i])
            for i, (a, into) in enumerate(
                ((keep, stay), (keep_st, stay_st), (move, mov.at[0, pl.ds(0, D)]), (move_st, line))
            )
        ]

    @pl.when(core == 0)
    def _():
        for copy in tables(src_e, src_s, dst_e, dst_s):
            copy.start()

    @pl.when(core == 1)
    def _():
        for copy in tables(dst_e, dst_s, src_e, src_s):
            copy.start()

    for copy in small:
        copy.start()

    def blk(by):
        return (b + by + N_BLK) % N_BLK

    ys = [(y + i) % 4 for i in range(4)]
    xcs = [(xc + i) % 8 for i in range(8)]
    xc_g, xc_b = [q % 4 for q in xcs], [(q // 4) * Z + z for q in xcs]

    def slice_peer(i):
        j, k = i // 8, i % 8
        return ys[j] * 8 + xcs[k], ys[j], (ys[j] * 4 + xc_g[k], xc_b[k])

    def z_peer(i):
        q = (z + i) % Z
        return q, q, (g, x_hi * Z + q)

    def y_peer(i):
        return ys[i], ys[i], (ys[i] * 4 + g % 4, b)

    slice_order = tuple(range(1, 32))
    z_order = (8, 7, 9, 6, 10, 5, 11, 4, 12, 3, 13, 2, 14, 1, 15)
    y_order = (2, 1, 3)
    up = 1 - 2 * core

    barrier = pltpu.get_barrier_semaphore()

    def greet(device):
        pl.semaphore_signal(barrier, inc=1, device_id=device, device_id_type=MESH)

    for i in slice_order:
        greet(slice_peer(i)[2])
    for i in z_order:
        greet(z_peer(i)[2])
    greet((g, blk(-up)))
    greet((g, blk(7 * up)))
    n_peers = len(slice_order) + len(z_order) + 2

    for copy in small:
        copy.wait()

    for k in range(ROUNDS):
        packed[k, 0:1, :] = s_ids[k : k + 1, :]
        packed[k, 1:2, :] = d_ids[k : k + 1, :]
        packed[k, 2:3, :] = r_ids[k : k + 1, :]
        packed[k, 3:4, :] = jnp.concatenate([n_ids[k : k + 1, :], jnp.full((1, ROWS - NEG), -1, jnp.int32)], axis=1)
        packed[k, 4:8, :] = jnp.full((4, ROWS), lengths[k], jnp.int32)

    wide = jnp.concatenate([rel[...], jnp.zeros((NREL, 512 - D), f32)], axis=1)
    wide = jnp.concatenate([wide, jnp.zeros((ROWS - NREL, 512), f32)], axis=0)
    rel_t[...] = wide.T[:D, :]
    for copy in tables(src_e, src_s, dst_e, dst_s):
        copy.wait()
    mov[0, STATE : STATE + 8, :] = jnp.broadcast_to(line[...], (8, ROWS))
    rg[...] = jnp.zeros_like(rg)

    def moved_copy(k, c):
        rows = pl.ds(CHUNKS[c][0], CHUNKS[c][1] + (8 if c == NC - 1 else 0))
        return pltpu.make_async_remote_copy(
            src_ref=mov.at[k, rows],
            dst_ref=mov.at[jnp.minimum(k + 1, ROUNDS - 1), rows],
            send_sem=send_sem.at[k, c],
            recv_sem=recv_sem.at[jnp.minimum(k + 1, ROUNDS - 1), c],
            device_id=(g, blk(up)),
            device_id_type=MESH,
        )

    def arrived(k, c):
        rows = pl.ds(CHUNKS[c][0], CHUNKS[c][1] + (8 if c == NC - 1 else 0))
        pltpu.make_async_remote_copy(
            src_ref=mov.at[k, rows],
            dst_ref=mov.at[k, rows],
            send_sem=send_sem.at[k, c],
            recv_sem=recv_sem.at[k, c],
            device_id=(g, blk(up)),
            device_id_type=MESH,
        ).wait_recv()

    def home_copy(c):
        rows = pl.ds(*HOME[c])
        return pltpu.make_async_remote_copy(
            src_ref=mov.at[ROUNDS - 1, rows],
            dst_ref=home.at[rows],
            send_sem=send_sem.at[ROUNDS - 1, c],
            recv_sem=back_sem.at[c],
            device_id=(g, blk(-7 * up)),
            device_id_type=MESH,
        )

    def home_state_copy():
        return pltpu.make_async_remote_copy(
            src_ref=mov.at[ROUNDS - 1, pl.ds(STATE, 8)],
            dst_ref=home_st,
            send_sem=send_sem.at[ROUNDS - 1, NH],
            recv_sem=back_sem.at[NH],
            device_id=(g, blk(-7 * up)),
            device_id_type=MESH,
        )

    def stepped(k, grad):
        state = mov[k, STATE : STATE + 8, :] + jnp.sum(grad * grad, axis=0, keepdims=True) * (1.0 / D)
        scale = (learn_rate / (jnp.sqrt(state) + epsilon))[0:1]
        mov[k, STATE : STATE + 8, :] = state
        for c, (r0, n) in enumerate(CHUNKS):
            mov[k, r0 : r0 + n, :] = mov[k, r0 : r0 + n, :] - grad[r0 : r0 + n] * scale

            @pl.when(k < ROUNDS - 1)
            def _():
                moved_copy(k, c).start()

    def settled(grad):
        new = stay_st[...] + jnp.sum(grad * grad, axis=0, keepdims=True) * (1.0 / D)
        stay_st[...] = new
        stay[...] = stay[...] - grad * (learn_rate / (jnp.sqrt(new) + epsilon))

    def related(h, tile):
        hot = (lax.broadcasted_iota(jnp.int32, (16, ROWS), 0) == tile[2:3]).astype(f32).astype(bf16)
        rg[:, :D] = rg[:, :D] + nt(jnp.concatenate([hot, hot], axis=1), both(s_buf[...] * h))

    def coefficients(tile):
        rows = sub_iota()
        valid = (lax.broadcasted_iota(jnp.int32, (1, ROWS), 1) < tile[4:5]).astype(f32)
        hit = (rows == tile[1:2]).astype(f32)
        count = jnp.sum((rows == tile[3:4]).astype(f32), axis=1, keepdims=True)
        return (count + hit) * valid, hit * valid

    def one_hot2(row):
        hot = (sub_iota() == row).astype(f32).astype(bf16)
        return jnp.concatenate([hot, hot], axis=1)

    def quadrants(x):
        return (x[:ROWS, :ROWS] + x[ROWS:, ROWS:]) + (x[:ROWS, ROWS:] + x[ROWS:, :ROWS])

    def two_by_two(hi, lo):
        line = jnp.concatenate([hi, lo], axis=1)
        return jnp.concatenate([line, line], axis=0)

    def two_by_two_t(hi, lo):
        return jnp.concatenate([jnp.concatenate([hi, hi], axis=1), jnp.concatenate([lo, lo], axis=1)], axis=0)

    def split_into(ref, r0, n, x):
        hi, lo = halves(x)
        ref[r0 : r0 + n, :ROWS] = hi
        ref[r0 : r0 + n, ROWS:] = lo

    def transposed_into(x):
        hi, lo = halves(x.T)
        fixed_t[:ROWS, :] = hi
        fixed_t[ROWS:, :] = lo

    def both(x):
        return jnp.concatenate(halves(x), axis=1)

    @pl.when(core == 0)
    def _():
        def prepare(k):
            tile = packed[k]
            w = picked(rel_t[...], tile[2:3])
            s = picked(stay[...], tile[0:1])
            a = s * w
            w_buf[...] = w
            s_buf[...] = s
            split_into(a2, 0, D, a)
            transposed_into(a)
            c, v = coefficients(tile)
            c1[...] = c.T
            dv[...] = v.T

        prepare(0)
        pl.semaphore_wait(barrier, n_peers)

        @pl.loop(0, ROUNDS)
        def _(k):
            total = jnp.zeros((2 * ROWS, 2 * ROWS), f32)
            for c, (r0, n) in enumerate(CHUNKS):

                @pl.when(k > 0)
                def _():
                    arrived(k, c)

                split_into(d2, r0, n, mov[k, r0 : r0 + n, :])
                total = total + nn(fixed_t[:, r0 : r0 + n], d2[r0 : r0 + n, :])
            m = c1[...] * jax.nn.sigmoid(quadrants(total)) - dv[...]
            hi, lo = halves(m)
            stepped(k, folded(nn(a2[...], two_by_two(hi, lo))))

            h = folded(nt(d2[...], two_by_two_t(hi, lo)))
            tile = packed[k]
            related(h, tile)
            settled(nt(both(w_buf[...] * h), one_hot2(tile[0:1])))

            @pl.when(k < ROUNDS - 1)
            def _():
                prepare(k + 1)

    @pl.when(core == 1)
    def _():
        for k in range(2, ROUNDS):
            greet((g, blk(k)))
        gotten[0] = packed[0]

        def id_copy(k):
            return pltpu.make_async_remote_copy(
                src_ref=packed.at[k],
                dst_ref=gotten.at[k],
                send_sem=id_send.at[k],
                recv_sem=id_recv.at[k],
                device_id=(g, blk(-k)),
                device_id_type=MESH,
            )

        def prepare(k):
            tile = gotten[k]
            w_buf[...] = picked(rel_t[...], tile[2:3])
            d = stay[...]
            split_into(d2, 0, D, d)
            transposed_into(d)
            c, v = coefficients(tile)
            c1[...] = c
            dv[...] = v

        prepare(0)
        pl.semaphore_wait(barrier, n_peers + ROUNDS - 2)
        for k in range(1, ROUNDS):
            id_copy(k).start()

        @pl.loop(0, ROUNDS)
        def _(k):
            tile = gotten[k]
            total = jnp.zeros((2 * ROWS, 2 * ROWS), f32)
            for c, (r0, n) in enumerate(CHUNKS):

                @pl.when(k > 0)
                def _():
                    arrived(k, c)

                s = picked(mov[k, r0 : r0 + n, :], tile[0:1])
                s_buf[r0 : r0 + n, :] = s
                split_into(a2, r0, n, s * w_buf[r0 : r0 + n, :])
                total = total + nn(fixed_t[:, r0 : r0 + n], a2[r0 : r0 + n, :])
            m = c1[...] * jax.nn.sigmoid(quadrants(total)) - dv[...]
            hi, lo = halves(m)
            h = folded(nn(d2[...], two_by_two(hi, lo)))
            grad = nt(both(w_buf[...] * h), one_hot2(tile[0:1]))
            stepped(k, grad)

            related(h, tile)
            settled(folded(nt(a2[...], two_by_two_t(hi, lo))))

            @pl.when(k < ROUNDS - 1)
            def _():
                id_copy(k + 1).wait_recv()
                prepare(k + 1)

        for k in range(1, ROUNDS):
            id_copy(k).wait_send()

    for q in range(4):
        tiles[q] = rg[:NREL, q * ROWS : (q + 1) * ROWS]

    def exchange(stage, peer, order, source, buf):
        def copy(i, slot):
            _, part, device = peer(i)
            return pltpu.make_async_remote_copy(
                src_ref=source(part),
                dst_ref=buf.at[slot],
                send_sem=ar_send.at[stage, i],
                recv_sem=ar_recv.at[stage, slot],
                device_id=device,
                device_id_type=MESH,
            )

        mine = peer(0)[0]
        for i in order:
            copy(i, mine).start()

        def wait_recv():
            for i in order:
                copy(i, peer(i)[0]).wait_recv()

        def wait_send():
            for i in order:
                copy(i, mine).wait_send()

        return wait_recv, wait_send

    def go_home(parts):
        for c in parts:
            if c == NH:
                home_state_copy().start()
            else:
                home_copy(c).start()

    def added(buf, n):
        value = buf[0]
        for q in range(1, n):
            value = value + buf[q]
        return value

    r1[y * 8 + xc] = tiles[y]
    received, sent1 = exchange(0, slice_peer, slice_order, lambda part: tiles.at[part], r1)
    go_home(PART1)
    received()
    r2[z] = added(r1, 32)
    received, sent2 = exchange(1, z_peer, z_order, lambda part: r2.at[z], r2)
    go_home(PART2)
    received()
    r3[y] = added(r2, Z)
    received, sent3 = exchange(2, y_peer, y_order, lambda part: r3.at[y], r3)
    go_home(PART3)
    received()

    square = r3[0] * r3[0]
    for q in range(1, 4):
        square = square + r3[q] * r3[q]
    old = jnp.zeros((NREL, 1), f32)
    which = lax.broadcasted_iota(jnp.int32, (NREL, 1), 0)
    for r in range(NREL):
        old = jnp.where(which == r, rel_state[r], old)
    rstate = old + jnp.sum(square, axis=1, keepdims=True) * (1.0 / D)
    scale = rel_rate / (jnp.sqrt(rstate) + epsilon)
    for q in range(4):
        lo, hi = q * ROWS, min(D, (q + 1) * ROWS)
        rel_o[:, lo:hi] = rel[:, lo:hi] - r3[q][:, : hi - lo] * scale

    for sent in (sent1, sent2, sent3):
        sent()

    @pl.loop(0, ROUNDS - 1)
    def _(k):
        for c in range(NC):
            moved_copy(k, c).wait_send()

    for c in range(NH):
        home_copy(c).wait_send()
    home_state_copy().wait_send()
    for c in range(NH):
        home_copy(c).wait_recv()
    home_state_copy().wait_recv()


def placed_back(stay, stay_st, home, home_st, rel_v, src_o, src_so, dst_o, dst_so, rel_o, sem):
    def copies(keep, keep_st, move, move_st):
        return [
            pltpu.make_async_copy(a, into, sem.at[i])
            for i, (a, into) in enumerate(
                (
                    (stay, keep),
                    (home, move),
                    (stay_st, keep_st),
                    (home_st.at[pl.ds(0, 1)], move_st),
                    (rel_v, rel_o),
                )
            )
        ]

    core = lax.axis_index("grp") % 2

    @pl.when(core == 0)
    def _():
        for copy in copies(src_o, src_so, dst_o, dst_so):
            copy.start()

    @pl.when(core == 1)
    def _():
        for copy in copies(dst_o, dst_so, src_o, src_so):
            copy.start()

    for copy in copies(src_o, src_so, dst_o, dst_so):
        copy.wait()


def local(src_emb, src_state, dst_emb, dst_state, relations, rel_state, src_ids, dst_ids, rel_ids, neg_ids, lengths):
    vmem, hbm = pl.BlockSpec(memory_space=pltpu.VMEM), pl.BlockSpec(memory_space=pltpu.HBM)
    table, line = jax.ShapeDtypeStruct((D, ROWS), f32), jax.ShapeDtypeStruct((1, ROWS), f32)
    relation = jax.ShapeDtypeStruct((NREL, D), f32)
    ids = pltpu.VMEM((ROUNDS, ROWS), jnp.int32)
    results = pl.pallas_call(
        window,
        out_shape=[table, line, table, jax.ShapeDtypeStruct((8, ROWS), f32), relation],
        in_specs=[hbm] * 11,
        out_specs=[vmem] * 5,
        scratch_shapes=[
            pltpu.SMEM((ROUNDS,), jnp.int32),
            pltpu.SMEM((NREL,), f32),
            pltpu.VMEM((NREL, D), f32),
            ids,
            ids,
            ids,
            pltpu.VMEM((ROUNDS, NEG), jnp.int32),
            pltpu.VMEM((1, ROWS), f32),
            pltpu.VMEM((ROUNDS, MOVED, ROWS), f32),
            pltpu.VMEM((D, ROWS), f32),
            pltpu.VMEM((D, ROWS), f32),
            pltpu.VMEM((2 * ROWS, D), bf16),
            pltpu.VMEM((D, 2 * ROWS), bf16),
            pltpu.VMEM((D, 2 * ROWS), bf16),
            pltpu.VMEM((D, ROWS), f32),
            pltpu.VMEM((16, 512), f32),
            pltpu.VMEM((ROWS, ROWS), f32),
            pltpu.VMEM((ROWS, ROWS), f32),
            pltpu.VMEM((ROUNDS, 8, ROWS), jnp.int32),
            pltpu.VMEM((ROUNDS, 8, ROWS), jnp.int32),
            pltpu.VMEM((4, 8, ROWS), f32),
            pltpu.VMEM((32, 8, ROWS), f32),
            pltpu.VMEM((Z, 8, ROWS), f32),
            pltpu.VMEM((4, 8, ROWS), f32),
            pltpu.SemaphoreType.DMA((11,)),
            pltpu.SemaphoreType.DMA((ROUNDS, max(NC, NH + 1))),
            pltpu.SemaphoreType.DMA((ROUNDS, NC)),
            pltpu.SemaphoreType.DMA((NH + 1,)),
            pltpu.SemaphoreType.DMA((ROUNDS,)),
            pltpu.SemaphoreType.DMA((ROUNDS,)),
            pltpu.SemaphoreType.DMA((3, 32)),
            pltpu.SemaphoreType.DMA((3, 32)),
        ],
        compiler_params=pltpu.CompilerParams(
            collective_id=0, has_side_effects=True, vmem_limit_bytes=60 * 1024 * 1024
        ),
    )(
        lengths,
        rel_state,
        src_emb,
        src_state.reshape(1, ROWS),
        dst_emb,
        dst_state.reshape(1, ROWS),
        relations,
        src_ids,
        dst_ids,
        rel_ids,
        neg_ids,
    )
    outs = pl.pallas_call(
        placed_back,
        out_shape=[table, line, table, line, relation],
        in_specs=[vmem] * 5,
        out_specs=[hbm] * 5,
        scratch_shapes=[pltpu.SemaphoreType.DMA((5,))],
    )(*results)
    return (outs[0], outs[1].reshape(ROWS), outs[2], outs[3].reshape(ROWS), outs[4])


def solution(mesh):
    both = ("grp", "blk")
    placed = (
        P(None, both),
        P(both),
        P(None, both),
        P(both),
        P(),
        P(),
        P(both, None),
        P(both, None),
        P(both, None),
        P(both, None),
        P(both),
    )
    return jax.shard_map(
        local,
        mesh=mesh,
        in_specs=placed,
        out_specs=(P(None, both), P(both), P(None, both), P(both), P()),
        check_vma=False,
    )
```

```python
import jax
import jax.numpy as jnp
from jax import lax
from jax.experimental import pallas as pl
from jax.experimental.pallas import tpu as pltpu
from jax.sharding import PartitionSpec as P

learn_rate = 0.1
rel_rate = 0.5
epsilon = 1e-08

D = 400
NREL = 8
ROWS = 128
NEG = 64
ROUNDS = 8
N_GRP = 16
N_BLK = 32
Z = 16

CHUNKS = ((0, 128), (128, 128), (256, 144))
NC = len(CHUNKS)
HOME = ((0, 200), (200, 200))
NH = len(HOME)
EARLY, MIDDLE = (0, 3), (3, 16)
STATE = D
MOVED = D + 8
MESH = pl.DeviceIdType.MESH
f32, bf16 = jnp.float32, jnp.bfloat16


def halves(x):
    hi = x.astype(bf16)
    return hi, (x - hi.astype(f32)).astype(bf16)


def nn(a, b):
    return lax.dot_general(a, b, (((1,), (0,)), ((), ())), preferred_element_type=f32)


def nt(a, b):
    return lax.dot_general(a, b, (((1,), (1,)), ((), ())), preferred_element_type=f32)


def folded(x):
    return x[:, :ROWS] + x[:, ROWS:]


def picked(table, row):
    index = jnp.broadcast_to(row, table.shape)
    return jnp.take_along_axis(table, index, axis=1, mode="promise_in_bounds")


def sub_iota():
    return lax.broadcasted_iota(jnp.int32, (ROWS, ROWS), 0)


def window(
    lengths_h,
    rel_state_h,
    src_e,
    src_s,
    dst_e,
    dst_s,
    rel_h,
    s_ids_h,
    d_ids_h,
    r_ids_h,
    n_ids_h,
    stay,
    stay_st,
    home,
    home_st,
    rel_o,
    lengths,
    rel_state,
    rel,
    s_ids,
    d_ids,
    r_ids,
    n_ids,
    line,
    mov,
    w_buf,
    s_buf,
    fixed_t,
    a2,
    d2,
    rel_t,
    rg,
    c1,
    dv,
    packed,
    gotten,
    tiles,
    r1,
    r2,
    r3,
    in_sem,
    send_sem,
    recv_sem,
    back_sem,
    id_send,
    id_recv,
    ar_send,
    ar_recv,
):
    g, b = lax.axis_index("grp"), lax.axis_index("blk")
    y, xc, core = g // 4, (b // Z) * 4 + g % 4, g % 2
    x_hi, z = b // Z, b % Z

    def blk(by):
        return (b + by + N_BLK) % N_BLK

    ys = [(y + i) % 4 for i in range(4)]
    xcs = [(xc + i) % 8 for i in range(8)]
    xc_g, xc_b = [q % 4 for q in xcs], [(q // 4) * Z + z for q in xcs]

    def slice_peer(i):
        j, k = i // 8, i % 8
        return ys[j] * 8 + xcs[k], ys[j], (ys[j] * 4 + xc_g[k], xc_b[k])

    def z_peer(i):
        q = (z + i) % Z
        return q, q, (g, x_hi * Z + q)

    def y_peer(i):
        return ys[i], ys[i], (ys[i] * 4 + g % 4, b)

    slice_order = tuple(range(1, 32))
    z_order = (8, 7, 9, 6, 10, 5, 11, 4, 12, 3, 13, 2, 14, 1, 15)
    y_order = (2, 1, 3)
    up = 1 - 2 * core

    barrier = pltpu.get_barrier_semaphore()

    def greet(device):
        pl.semaphore_signal(barrier, inc=1, device_id=device, device_id_type=MESH)

    for i in z_order:
        greet(z_peer(i)[2])
    for i in slice_order:
        greet(slice_peer(i)[2])
    greet((g, blk(-up)))
    greet((g, blk(7 * up)))
    small = [
        pltpu.make_async_copy(a, into, in_sem.at[i])
        for i, (a, into) in enumerate(
            (
                (r_ids_h, r_ids),
                (s_ids_h, s_ids),
                (rel_h, rel),
                (d_ids_h, d_ids),
                (n_ids_h, n_ids),
                (lengths_h, lengths),
                (rel_state_h, rel_state),
            )
        )
    ]
    n_small = len(small)

    def tables(keep, keep_st, move, move_st):
        return [
            pltpu.make_async_copy(a, into, in_sem.at[n_small + i])
            for i, (a, into) in enumerate(
                ((keep, stay), (keep_st, stay_st), (move, mov.at[0, pl.ds(0, D)]), (move_st, line))
            )
        ]

    @pl.when(core == 0)
    def _():
        for copy in tables(src_e, src_s, dst_e, dst_s):
            copy.start()

    @pl.when(core == 1)
    def _():
        for copy in tables(dst_e, dst_s, src_e, src_s):
            copy.start()

    for copy in small:
        copy.start()

    n_peers = len(slice_order) + len(z_order) + 2

    for copy in small:
        copy.wait()

    for k in range(ROUNDS):
        packed[k, 0:1, :] = s_ids[k : k + 1, :]
        packed[k, 1:2, :] = d_ids[k : k + 1, :]
        packed[k, 2:3, :] = r_ids[k : k + 1, :]
        packed[k, 3:4, :] = jnp.concatenate([n_ids[k : k + 1, :], jnp.full((1, ROWS - NEG), -1, jnp.int32)], axis=1)
        packed[k, 4:8, :] = jnp.full((4, ROWS), lengths[k], jnp.int32)

    wide = jnp.concatenate([rel[...], jnp.zeros((NREL, 512 - D), f32)], axis=1)
    wide = jnp.concatenate([wide, jnp.zeros((ROWS - NREL, 512), f32)], axis=0)
    rel_t[...] = wide.T[:D, :]
    for copy in tables(src_e, src_s, dst_e, dst_s):
        copy.wait()
    mov[0, STATE : STATE + 8, :] = jnp.broadcast_to(line[...], (8, ROWS))
    rg[...] = jnp.zeros_like(rg)

    def moved_copy(k, c):
        rows = pl.ds(CHUNKS[c][0], CHUNKS[c][1] + (8 if c == NC - 1 else 0))
        return pltpu.make_async_remote_copy(
            src_ref=mov.at[k, rows],
            dst_ref=mov.at[jnp.minimum(k + 1, ROUNDS - 1), rows],
            send_sem=send_sem.at[k, c],
            recv_sem=recv_sem.at[jnp.minimum(k + 1, ROUNDS - 1), c],
            device_id=(g, blk(up)),
            device_id_type=MESH,
        )

    def arrived(k, c):
        rows = pl.ds(CHUNKS[c][0], CHUNKS[c][1] + (8 if c == NC - 1 else 0))
        pltpu.make_async_remote_copy(
            src_ref=mov.at[k, rows],
            dst_ref=mov.at[k, rows],
            send_sem=send_sem.at[k, c],
            recv_sem=recv_sem.at[k, c],
            device_id=(g, blk(up)),
            device_id_type=MESH,
        ).wait_recv()

    def home_copy(c):
        rows = pl.ds(*HOME[c])
        return pltpu.make_async_remote_copy(
            src_ref=mov.at[ROUNDS - 1, rows],
            dst_ref=home.at[rows],
            send_sem=send_sem.at[ROUNDS - 1, c],
            recv_sem=back_sem.at[c],
            device_id=(g, blk(-7 * up)),
            device_id_type=MESH,
        )

    def home_state_copy():
        return pltpu.make_async_remote_copy(
            src_ref=mov.at[ROUNDS - 1, pl.ds(STATE, 8)],
            dst_ref=home_st,
            send_sem=send_sem.at[ROUNDS - 1, NH],
            recv_sem=back_sem.at[NH],
            device_id=(g, blk(-7 * up)),
            device_id_type=MESH,
        )

    def stepped(k, grad):
        state = mov[k, STATE : STATE + 8, :] + jnp.sum(grad * grad, axis=0, keepdims=True) * (1.0 / D)
        scale = (learn_rate / (jnp.sqrt(state) + epsilon))[0:1]
        mov[k, STATE : STATE + 8, :] = state
        for c, (r0, n) in enumerate(CHUNKS):
            mov[k, r0 : r0 + n, :] = mov[k, r0 : r0 + n, :] - grad[r0 : r0 + n] * scale

            @pl.when(k < ROUNDS - 1)
            def _():
                moved_copy(k, c).start()

    def settled(grad):
        new = stay_st[...] + jnp.sum(grad * grad, axis=0, keepdims=True) * (1.0 / D)
        stay_st[...] = new
        stay[...] = stay[...] - grad * (learn_rate / (jnp.sqrt(new) + epsilon))

    def related(h, tile):
        hot = (lax.broadcasted_iota(jnp.int32, (16, ROWS), 0) == tile[2:3]).astype(f32).astype(bf16)
        rg[:, :D] = rg[:, :D] + nt(jnp.concatenate([hot, hot], axis=1), both(s_buf[...] * h))

    def coefficients(tile):
        rows = sub_iota()
        valid = (lax.broadcasted_iota(jnp.int32, (1, ROWS), 1) < tile[4:5]).astype(f32)
        hit = (rows == tile[1:2]).astype(f32)
        count = jnp.sum((rows == tile[3:4]).astype(f32), axis=1, keepdims=True)
        return (count + hit) * valid, hit * valid

    def one_hot2(row):
        hot = (sub_iota() == row).astype(f32).astype(bf16)
        return jnp.concatenate([hot, hot], axis=1)

    def quadrants(x):
        return (x[:ROWS, :ROWS] + x[ROWS:, ROWS:]) + (x[:ROWS, ROWS:] + x[ROWS:, :ROWS])

    def two_by_two(hi, lo):
        line = jnp.concatenate([hi, lo], axis=1)
        return jnp.concatenate([line, line], axis=0)

    def two_by_two_t(hi, lo):
        return jnp.concatenate([jnp.concatenate([hi, hi], axis=1), jnp.concatenate([lo, lo], axis=1)], axis=0)

    def split_into(ref, r0, n, x):
        hi, lo = halves(x)
        ref[r0 : r0 + n, :ROWS] = hi
        ref[r0 : r0 + n, ROWS:] = lo

    def transposed_into(x):
        hi, lo = halves(x.T)
        fixed_t[:ROWS, :] = hi
        fixed_t[ROWS:, :] = lo

    def both(x):
        return jnp.concatenate(halves(x), axis=1)

    @pl.when(core == 0)
    def _():
        def prepare(k):
            tile = packed[k]
            w = picked(rel_t[...], tile[2:3])
            s = picked(stay[...], tile[0:1])
            a = s * w
            w_buf[...] = w
            s_buf[...] = s
            split_into(a2, 0, D, a)
            transposed_into(a)
            c, v = coefficients(tile)
            c1[...] = c.T
            dv[...] = v.T

        prepare(0)
        pl.semaphore_wait(barrier, n_peers)

        @pl.loop(0, ROUNDS)
        def _(k):
            total = jnp.zeros((2 * ROWS, 2 * ROWS), f32)
            for c, (r0, n) in enumerate(CHUNKS):

                @pl.when(k > 0)
                def _():
                    arrived(k, c)

                split_into(d2, r0, n, mov[k, r0 : r0 + n, :])
                total = total + nn(fixed_t[:, r0 : r0 + n], d2[r0 : r0 + n, :])
            m = c1[...] * jax.nn.sigmoid(quadrants(total)) - dv[...]
            hi, lo = halves(m)
            stepped(k, folded(nn(a2[...], two_by_two(hi, lo))))

            h = folded(nt(d2[...], two_by_two_t(hi, lo)))
            tile = packed[k]
            related(h, tile)
            settled(nt(both(w_buf[...] * h), one_hot2(tile[0:1])))

            @pl.when(k < ROUNDS - 1)
            def _():
                prepare(k + 1)

    @pl.when(core == 1)
    def _():
        for k in range(2, ROUNDS):
            greet((g, blk(k)))
        gotten[0] = packed[0]

        def id_copy(k):
            return pltpu.make_async_remote_copy(
                src_ref=packed.at[k],
                dst_ref=gotten.at[k],
                send_sem=id_send.at[k],
                recv_sem=id_recv.at[k],
                device_id=(g, blk(-k)),
                device_id_type=MESH,
            )

        def prepare(k):
            tile = gotten[k]
            w_buf[...] = picked(rel_t[...], tile[2:3])
            d = stay[...]
            split_into(d2, 0, D, d)
            transposed_into(d)
            c, v = coefficients(tile)
            c1[...] = c
            dv[...] = v

        prepare(0)
        pl.semaphore_wait(barrier, n_peers + ROUNDS - 2)
        for k in range(1, ROUNDS):
            id_copy(k).start()

        @pl.loop(0, ROUNDS)
        def _(k):
            tile = gotten[k]
            total = jnp.zeros((2 * ROWS, 2 * ROWS), f32)
            for c, (r0, n) in enumerate(CHUNKS):

                @pl.when(k > 0)
                def _():
                    arrived(k, c)

                s = picked(mov[k, r0 : r0 + n, :], tile[0:1])
                s_buf[r0 : r0 + n, :] = s
                split_into(a2, r0, n, s * w_buf[r0 : r0 + n, :])
                total = total + nn(fixed_t[:, r0 : r0 + n], a2[r0 : r0 + n, :])
            m = c1[...] * jax.nn.sigmoid(quadrants(total)) - dv[...]
            hi, lo = halves(m)
            h = folded(nn(d2[...], two_by_two(hi, lo)))
            grad = nt(both(w_buf[...] * h), one_hot2(tile[0:1]))
            stepped(k, grad)

            related(h, tile)
            settled(folded(nt(a2[...], two_by_two_t(hi, lo))))

            @pl.when(k < ROUNDS - 1)
            def _():
                id_copy(k + 1).wait_recv()
                prepare(k + 1)

        for k in range(1, ROUNDS):
            id_copy(k).wait_send()

    for q in range(4):
        tiles[q] = rg[:NREL, q * ROWS : (q + 1) * ROWS]

    def exchange(stage, peer, order, source, buf):
        def copy(i, slot):
            _, part, device = peer(i)
            return pltpu.make_async_remote_copy(
                src_ref=source(part),
                dst_ref=buf.at[slot],
                send_sem=ar_send.at[stage, i],
                recv_sem=ar_recv.at[stage, slot],
                device_id=device,
                device_id_type=MESH,
            )

        mine = peer(0)[0]
        for i in order:
            copy(i, mine).start()

        def wait_recv():
            for i in order:
                copy(i, peer(i)[0]).wait_recv()

        def wait_send():
            for i in order:
                copy(i, mine).wait_send()

        return wait_recv, wait_send

    home_z = (z + Z - 7 * up) % Z

    def go_home(turn):
        early = (home_z >= EARLY[0]) & (home_z < EARLY[1])
        middle = (home_z >= MIDDLE[0]) & (home_z < MIDDLE[1])
        now = (early, middle, jnp.logical_not(early | middle))[turn]

        @pl.when(now)
        def _():
            home_state_copy().start()
            for c in range(NH):
                home_copy(c).start()

    def added(buf, n):
        value = buf[0]
        for q in range(1, n):
            value = value + buf[q]
        return value

    r1[y * 8 + xc] = tiles[y]
    received, sent1 = exchange(0, slice_peer, slice_order, lambda part: tiles.at[part], r1)
    go_home(0)
    received()
    r2[z] = added(r1, 32)
    received, sent2 = exchange(1, z_peer, z_order, lambda part: r2.at[z], r2)
    go_home(1)
    received()
    r3[y] = added(r2, Z)
    received, sent3 = exchange(2, y_peer, y_order, lambda part: r3.at[y], r3)
    go_home(2)
    received()

    square = r3[0] * r3[0]
    for q in range(1, 4):
        square = square + r3[q] * r3[q]
    old = jnp.zeros((NREL, 1), f32)
    which = lax.broadcasted_iota(jnp.int32, (NREL, 1), 0)
    for r in range(NREL):
        old = jnp.where(which == r, rel_state[r], old)
    rstate = old + jnp.sum(square, axis=1, keepdims=True) * (1.0 / D)
    scale = rel_rate / (jnp.sqrt(rstate) + epsilon)
    for q in range(4):
        lo, hi = q * ROWS, min(D, (q + 1) * ROWS)
        rel_o[:, lo:hi] = rel[:, lo:hi] - r3[q][:, : hi - lo] * scale

    for sent in (sent1, sent2, sent3):
        sent()

    @pl.loop(0, ROUNDS - 1)
    def _(k):
        for c in range(NC):
            moved_copy(k, c).wait_send()

    for c in range(NH):
        home_copy(c).wait_send()
    home_state_copy().wait_send()
    for c in range(NH):
        home_copy(c).wait_recv()
    home_state_copy().wait_recv()


def placed_back(stay, stay_st, home, home_st, rel_v, src_o, src_so, dst_o, dst_so, rel_o, sem):
    def copies(keep, keep_st, move, move_st):
        return [
            pltpu.make_async_copy(a, into, sem.at[i])
            for i, (a, into) in enumerate(
                (
                    (stay, keep),
                    (home, move),
                    (stay_st, keep_st),
                    (home_st.at[pl.ds(0, 1)], move_st),
                    (rel_v, rel_o),
                )
            )
        ]

    core = lax.axis_index("grp") % 2

    @pl.when(core == 0)
    def _():
        for copy in copies(src_o, src_so, dst_o, dst_so):
            copy.start()

    @pl.when(core == 1)
    def _():
        for copy in copies(dst_o, dst_so, src_o, src_so):
            copy.start()

    for copy in copies(src_o, src_so, dst_o, dst_so):
        copy.wait()


def local(src_emb, src_state, dst_emb, dst_state, relations, rel_state, src_ids, dst_ids, rel_ids, neg_ids, lengths):
    vmem, hbm = pl.BlockSpec(memory_space=pltpu.VMEM), pl.BlockSpec(memory_space=pltpu.HBM)
    table, line = jax.ShapeDtypeStruct((D, ROWS), f32), jax.ShapeDtypeStruct((1, ROWS), f32)
    relation = jax.ShapeDtypeStruct((NREL, D), f32)
    ids = pltpu.VMEM((ROUNDS, ROWS), jnp.int32)
    results = pl.pallas_call(
        window,
        out_shape=[table, line, table, jax.ShapeDtypeStruct((8, ROWS), f32), relation],
        in_specs=[hbm] * 11,
        out_specs=[vmem] * 5,
        scratch_shapes=[
            pltpu.SMEM((ROUNDS,), jnp.int32),
            pltpu.SMEM((NREL,), f32),
            pltpu.VMEM((NREL, D), f32),
            ids,
            ids,
            ids,
            pltpu.VMEM((ROUNDS, NEG), jnp.int32),
            pltpu.VMEM((1, ROWS), f32),
            pltpu.VMEM((ROUNDS, MOVED, ROWS), f32),
            pltpu.VMEM((D, ROWS), f32),
            pltpu.VMEM((D, ROWS), f32),
            pltpu.VMEM((2 * ROWS, D), bf16),
            pltpu.VMEM((D, 2 * ROWS), bf16),
            pltpu.VMEM((D, 2 * ROWS), bf16),
            pltpu.VMEM((D, ROWS), f32),
            pltpu.VMEM((16, 512), f32),
            pltpu.VMEM((ROWS, ROWS), f32),
            pltpu.VMEM((ROWS, ROWS), f32),
            pltpu.VMEM((ROUNDS, 8, ROWS), jnp.int32),
            pltpu.VMEM((ROUNDS, 8, ROWS), jnp.int32),
            pltpu.VMEM((4, 8, ROWS), f32),
            pltpu.VMEM((32, 8, ROWS), f32),
            pltpu.VMEM((Z, 8, ROWS), f32),
            pltpu.VMEM((4, 8, ROWS), f32),
            pltpu.SemaphoreType.DMA((11,)),
            pltpu.SemaphoreType.DMA((ROUNDS, max(NC, NH + 1))),
            pltpu.SemaphoreType.DMA((ROUNDS, NC)),
            pltpu.SemaphoreType.DMA((NH + 1,)),
            pltpu.SemaphoreType.DMA((ROUNDS,)),
            pltpu.SemaphoreType.DMA((ROUNDS,)),
            pltpu.SemaphoreType.DMA((3, 32)),
            pltpu.SemaphoreType.DMA((3, 32)),
        ],
        compiler_params=pltpu.CompilerParams(
            collective_id=0, has_side_effects=True, vmem_limit_bytes=60 * 1024 * 1024
        ),
    )(
        lengths,
        rel_state,
        src_emb,
        src_state.reshape(1, ROWS),
        dst_emb,
        dst_state.reshape(1, ROWS),
        relations,
        src_ids,
        dst_ids,
        rel_ids,
        neg_ids,
    )
    outs = pl.pallas_call(
        placed_back,
        out_shape=[table, line, table, line, relation],
        in_specs=[vmem] * 5,
        out_specs=[hbm] * 5,
        scratch_shapes=[pltpu.SemaphoreType.DMA((5,))],
    )(*results)
    return (outs[0], outs[1].reshape(ROWS), outs[2], outs[3].reshape(ROWS), outs[4])


def solution(mesh):
    both = ("grp", "blk")
    placed = (
        P(None, both),
        P(both),
        P(None, both),
        P(both),
        P(),
        P(),
        P(both, None),
        P(both, None),
        P(both, None),
        P(both, None),
        P(both),
    )
    return jax.shard_map(
        local,
        mesh=mesh,
        in_specs=placed,
        out_specs=(P(None, both), P(both), P(None, both), P(both), P()),
        check_vma=False,
    )
```

```python
import jax
import jax.numpy as jnp
from jax import lax
from jax.experimental import pallas as pl
from jax.experimental.pallas import tpu as pltpu
from jax.sharding import PartitionSpec as P

learn_rate = 0.1
rel_rate = 0.5
epsilon = 1e-08

D = 400
NREL = 8
ROWS = 128
NEG = 64
ROUNDS = 8
N_GRP = 16
N_BLK = 32
Z = 16

CHUNKS = ((0, 128), (128, 128), (256, 144))
NC = len(CHUNKS)
HOME = ((0, 200), (200, 200))
NH = len(HOME)
EARLY, MIDDLE = (0, 3), (3, 16)
STATE = D
MOVED = D + 8
MESH = pl.DeviceIdType.MESH
f32, bf16 = jnp.float32, jnp.bfloat16


def halves(x):
    hi = x.astype(bf16)
    return hi, (x - hi.astype(f32)).astype(bf16)


def nn(a, b):
    return lax.dot_general(a, b, (((1,), (0,)), ((), ())), preferred_element_type=f32)


def nt(a, b):
    return lax.dot_general(a, b, (((1,), (1,)), ((), ())), preferred_element_type=f32)


def folded(x):
    return x[:, :ROWS] + x[:, ROWS:]


def picked(table, row):
    index = jnp.broadcast_to(row, table.shape)
    return jnp.take_along_axis(table, index, axis=1, mode="promise_in_bounds")


def sub_iota():
    return lax.broadcasted_iota(jnp.int32, (ROWS, ROWS), 0)


def window(
    lengths_h,
    rel_state_h,
    src_e,
    src_s,
    dst_e,
    dst_s,
    rel_h,
    s_ids_h,
    d_ids_h,
    r_ids_h,
    n_ids_h,
    stay,
    stay_st,
    home,
    home_st,
    rel_o,
    lengths,
    rel_state,
    rel,
    s_ids,
    d_ids,
    r_ids,
    n_ids,
    line,
    mov,
    w_buf,
    s_buf,
    fixed_t,
    a2,
    d2,
    m2,
    rel_t,
    rg,
    c1,
    dv,
    packed,
    gotten,
    tiles,
    r1,
    r2,
    r3,
    in_sem,
    send_sem,
    recv_sem,
    back_sem,
    id_send,
    id_recv,
    ar_send,
    ar_recv,
):
    g, b = lax.axis_index("grp"), lax.axis_index("blk")
    y, xc, core = g // 4, (b // Z) * 4 + g % 4, g % 2
    x_hi, z = b // Z, b % Z

    def blk(by):
        return (b + by + N_BLK) % N_BLK

    ys = [(y + i) % 4 for i in range(4)]
    xcs = [(xc + i) % 8 for i in range(8)]
    xc_g, xc_b = [q % 4 for q in xcs], [(q // 4) * Z + z for q in xcs]

    def slice_peer(i):
        j, k = i // 8, i % 8
        return ys[j] * 8 + xcs[k], ys[j], (ys[j] * 4 + xc_g[k], xc_b[k])

    def z_peer(i):
        q = (z + i) % Z
        return q, q, (g, x_hi * Z + q)

    def y_peer(i):
        return ys[i], ys[i], (ys[i] * 4 + g % 4, b)

    far_y, far_x = (0, 2, 4, 2), (0, 1, 2, 3, 4, 3, 2, 1)
    slice_order = sorted(range(1, 32), key=lambda i: -(far_y[i // 8] + far_x[i % 8]))
    z_order = (8, 7, 9, 6, 10, 5, 11, 4, 12, 3, 13, 2, 14, 1, 15)
    y_order = (2, 1, 3)
    up = 1 - 2 * core

    barrier = pltpu.get_barrier_semaphore()

    def greet(device):
        pl.semaphore_signal(barrier, inc=1, device_id=device, device_id_type=MESH)

    for i in z_order:
        greet(z_peer(i)[2])
    for i in slice_order:
        greet(slice_peer(i)[2])
    greet((g, blk(-up)))
    greet((g, blk(7 * up)))
    small = [
        pltpu.make_async_copy(a, into, in_sem.at[i])
        for i, (a, into) in enumerate(
            (
                (r_ids_h, r_ids),
                (s_ids_h, s_ids),
                (rel_h, rel),
                (d_ids_h, d_ids),
                (n_ids_h, n_ids),
                (lengths_h, lengths),
                (rel_state_h, rel_state),
            )
        )
    ]
    n_small = len(small)

    def tables(keep, keep_st, move, move_st):
        return [
            pltpu.make_async_copy(a, into, in_sem.at[n_small + i])
            for i, (a, into) in enumerate(
                ((keep, stay), (keep_st, stay_st), (move, mov.at[0, pl.ds(0, D)]), (move_st, line))
            )
        ]

    @pl.when(core == 0)
    def _():
        for copy in tables(src_e, src_s, dst_e, dst_s):
            copy.start()

    @pl.when(core == 1)
    def _():
        for copy in tables(dst_e, dst_s, src_e, src_s):
            copy.start()

    for copy in small:
        copy.start()

    n_peers = len(slice_order) + len(z_order) + 2

    for copy in small:
        copy.wait()

    for k in range(ROUNDS):
        packed[k, 0:1, :] = s_ids[k : k + 1, :]
        packed[k, 1:2, :] = d_ids[k : k + 1, :]
        packed[k, 2:3, :] = r_ids[k : k + 1, :]
        packed[k, 3:4, :] = jnp.concatenate([n_ids[k : k + 1, :], jnp.full((1, ROWS - NEG), -1, jnp.int32)], axis=1)
        packed[k, 4:8, :] = jnp.full((4, ROWS), lengths[k], jnp.int32)

    wide = jnp.concatenate([rel[...], jnp.zeros((NREL, 512 - D), f32)], axis=1)
    wide = jnp.concatenate([wide, jnp.zeros((ROWS - NREL, 512), f32)], axis=0)
    rel_t[...] = wide.T[:D, :]
    for copy in tables(src_e, src_s, dst_e, dst_s):
        copy.wait()
    mov[0, STATE : STATE + 8, :] = jnp.broadcast_to(line[...], (8, ROWS))
    rg[...] = jnp.zeros_like(rg)

    def moved_copy(k, c):
        rows = pl.ds(CHUNKS[c][0], CHUNKS[c][1] + (8 if c == NC - 1 else 0))
        return pltpu.make_async_remote_copy(
            src_ref=mov.at[k, rows],
            dst_ref=mov.at[jnp.minimum(k + 1, ROUNDS - 1), rows],
            send_sem=send_sem.at[k, c],
            recv_sem=recv_sem.at[jnp.minimum(k + 1, ROUNDS - 1), c],
            device_id=(g, blk(up)),
            device_id_type=MESH,
        )

    def arrived(k, c):
        rows = pl.ds(CHUNKS[c][0], CHUNKS[c][1] + (8 if c == NC - 1 else 0))
        pltpu.make_async_remote_copy(
            src_ref=mov.at[k, rows],
            dst_ref=mov.at[k, rows],
            send_sem=send_sem.at[k, c],
            recv_sem=recv_sem.at[k, c],
            device_id=(g, blk(up)),
            device_id_type=MESH,
        ).wait_recv()

    def home_copy(c):
        rows = pl.ds(*HOME[c])
        return pltpu.make_async_remote_copy(
            src_ref=mov.at[ROUNDS - 1, rows],
            dst_ref=home.at[rows],
            send_sem=send_sem.at[ROUNDS - 1, c],
            recv_sem=back_sem.at[c],
            device_id=(g, blk(-7 * up)),
            device_id_type=MESH,
        )

    def home_state_copy():
        return pltpu.make_async_remote_copy(
            src_ref=mov.at[ROUNDS - 1, pl.ds(STATE, 8)],
            dst_ref=home_st,
            send_sem=send_sem.at[ROUNDS - 1, NH],
            recv_sem=back_sem.at[NH],
            device_id=(g, blk(-7 * up)),
            device_id_type=MESH,
        )

    def stepped(k, grad):
        state = mov[k, STATE : STATE + 8, :] + jnp.sum(grad * grad, axis=0, keepdims=True) * (1.0 / D)
        scale = (learn_rate / (jnp.sqrt(state) + epsilon))[0:1]
        mov[k, STATE : STATE + 8, :] = state
        for c, (r0, n) in enumerate(CHUNKS):
            mov[k, r0 : r0 + n, :] = mov[k, r0 : r0 + n, :] - grad[r0 : r0 + n] * scale
            if not isinstance(k, int):
                moved_copy(k, c).start()

    def settled(grad):
        new = stay_st[...] + jnp.sum(grad * grad, axis=0, keepdims=True) * (1.0 / D)
        stay_st[...] = new
        stay[...] = stay[...] - grad * (learn_rate / (jnp.sqrt(new) + epsilon))

    def related(h, tile):
        hot = (lax.broadcasted_iota(jnp.int32, (16, ROWS), 0) == tile[2:3]).astype(f32).astype(bf16)
        rg[:, :D] = rg[:, :D] + nt(jnp.concatenate([hot, hot], axis=1), both(s_buf[...] * h))

    def coefficients(tile):
        rows = sub_iota()
        valid = (lax.broadcasted_iota(jnp.int32, (1, ROWS), 1) < tile[4:5]).astype(f32)
        hit = (rows == tile[1:2]).astype(f32)
        count = jnp.sum((rows == tile[3:4]).astype(f32), axis=1, keepdims=True)
        return (count + hit) * valid, hit * valid

    def one_hot2(row):
        hot = (sub_iota() == row).astype(f32).astype(bf16)
        return jnp.concatenate([hot, hot], axis=1)

    def quadrants(x):
        return (x[:ROWS, :ROWS] + x[ROWS:, ROWS:]) + (x[:ROWS, ROWS:] + x[ROWS:, :ROWS])

    def two_by_two(hi, lo):
        line = jnp.concatenate([hi, lo], axis=1)
        return jnp.concatenate([line, line], axis=0)

    def two_by_two_t(hi, lo):
        return jnp.concatenate([jnp.concatenate([hi, hi], axis=1), jnp.concatenate([lo, lo], axis=1)], axis=0)

    def split_into(ref, r0, n, x):
        hi, lo = halves(x)
        ref[r0 : r0 + n, :ROWS] = hi
        ref[r0 : r0 + n, ROWS:] = lo

    def transposed_into(x):
        hi, lo = halves(x.T)
        fixed_t[:ROWS, :] = hi
        fixed_t[ROWS:, :] = lo

    def left_over(hi, lo, h):
        m2[:, :ROWS] = hi
        m2[:, ROWS:] = lo
        w_buf[...] = w_buf[...] * h

    def both(x):
        return jnp.concatenate(halves(x), axis=1)

    @pl.when(core == 0)
    def _():
        def prepare(k):
            tile = packed[k]
            w = picked(rel_t[...], tile[2:3])
            s = picked(stay[...], tile[0:1])
            a = s * w
            w_buf[...] = w
            s_buf[...] = s
            split_into(a2, 0, D, a)
            transposed_into(a)
            c, v = coefficients(tile)
            c1[...] = c.T
            dv[...] = v.T

        prepare(0)
        pl.semaphore_wait(barrier, n_peers)

        @pl.loop(0, ROUNDS)
        def _(k):
            total = jnp.zeros((2 * ROWS, 2 * ROWS), f32)
            for c, (r0, n) in enumerate(CHUNKS):

                @pl.when(k > 0)
                def _():
                    arrived(k, c)

                split_into(d2, r0, n, mov[k, r0 : r0 + n, :])
                total = total + nn(fixed_t[:, r0 : r0 + n], d2[r0 : r0 + n, :])
            m = c1[...] * jax.nn.sigmoid(quadrants(total)) - dv[...]
            hi, lo = halves(m)

            @pl.when(k < ROUNDS - 1)
            def _():
                stepped(k, folded(nn(a2[...], two_by_two(hi, lo))))

            h = folded(nt(d2[...], two_by_two_t(hi, lo)))
            tile = packed[k]
            related(h, tile)

            @pl.when(k < ROUNDS - 1)
            def _():
                settled(nt(both(w_buf[...] * h), one_hot2(tile[0:1])))
                prepare(k + 1)

            @pl.when(k == ROUNDS - 1)
            def _():
                left_over(hi, lo, h)

    @pl.when(core == 1)
    def _():
        for k in range(2, ROUNDS):
            greet((g, blk(k)))
        gotten[0] = packed[0]

        def id_copy(k):
            return pltpu.make_async_remote_copy(
                src_ref=packed.at[k],
                dst_ref=gotten.at[k],
                send_sem=id_send.at[k],
                recv_sem=id_recv.at[k],
                device_id=(g, blk(-k)),
                device_id_type=MESH,
            )

        def prepare(k):
            tile = gotten[k]
            w_buf[...] = picked(rel_t[...], tile[2:3])
            d = stay[...]
            split_into(d2, 0, D, d)
            transposed_into(d)
            c, v = coefficients(tile)
            c1[...] = c
            dv[...] = v

        prepare(0)
        pl.semaphore_wait(barrier, n_peers + ROUNDS - 2)
        for k in range(1, ROUNDS):
            id_copy(k).start()

        @pl.loop(0, ROUNDS)
        def _(k):
            tile = gotten[k]
            total = jnp.zeros((2 * ROWS, 2 * ROWS), f32)
            for c, (r0, n) in enumerate(CHUNKS):

                @pl.when(k > 0)
                def _():
                    arrived(k, c)

                s = picked(mov[k, r0 : r0 + n, :], tile[0:1])
                s_buf[r0 : r0 + n, :] = s
                split_into(a2, r0, n, s * w_buf[r0 : r0 + n, :])
                total = total + nn(fixed_t[:, r0 : r0 + n], a2[r0 : r0 + n, :])
            m = c1[...] * jax.nn.sigmoid(quadrants(total)) - dv[...]
            hi, lo = halves(m)
            h = folded(nn(d2[...], two_by_two(hi, lo)))

            @pl.when(k < ROUNDS - 1)
            def _():
                stepped(k, nt(both(w_buf[...] * h), one_hot2(tile[0:1])))

            related(h, tile)

            @pl.when(k < ROUNDS - 1)
            def _():
                settled(folded(nt(a2[...], two_by_two_t(hi, lo))))
                id_copy(k + 1).wait_recv()
                prepare(k + 1)

            @pl.when(k == ROUNDS - 1)
            def _():
                left_over(hi, lo, h)

        for k in range(1, ROUNDS):
            id_copy(k).wait_send()

    for q in range(4):
        tiles[q] = rg[:NREL, q * ROWS : (q + 1) * ROWS]

    def exchange(stage, peer, order, source, buf):
        def copy(i, slot):
            _, part, device = peer(i)
            return pltpu.make_async_remote_copy(
                src_ref=source(part),
                dst_ref=buf.at[slot],
                send_sem=ar_send.at[stage, i],
                recv_sem=ar_recv.at[stage, slot],
                device_id=device,
                device_id_type=MESH,
            )

        mine = peer(0)[0]
        for i in order:
            copy(i, mine).start()

        def wait_recv():
            for i in order:
                copy(i, peer(i)[0]).wait_recv()

        def wait_send():
            for i in order:
                copy(i, mine).wait_send()

        return wait_recv, wait_send

    home_z = (z + Z - 7 * up) % Z

    def go_home(turn):
        early = (home_z >= EARLY[0]) & (home_z < EARLY[1])
        middle = (home_z >= MIDDLE[0]) & (home_z < MIDDLE[1])
        now = (early, middle, jnp.logical_not(early | middle))[turn]

        @pl.when(now)
        def _():
            home_state_copy().start()
            for c in range(NH):
                home_copy(c).start()

    def added(buf, n):
        value = buf[0]
        for q in range(1, n):
            value = value + buf[q]
        return value

    r1[y * 8 + xc] = tiles[y]
    received, sent1 = exchange(0, slice_peer, slice_order, lambda part: tiles.at[part], r1)

    hi, lo = m2[:, :ROWS], m2[:, ROWS:]
    last = ROUNDS - 1

    @pl.when(core == 0)
    def _():
        stepped(last, folded(nn(a2[...], two_by_two(hi, lo))))

    @pl.when(core == 1)
    def _():
        stepped(last, nt(both(w_buf[...]), one_hot2(gotten[last, 0:1])))

    go_home(0)

    @pl.when(core == 0)
    def _():
        settled(nt(both(w_buf[...]), one_hot2(packed[last, 0:1])))

    @pl.when(core == 1)
    def _():
        settled(folded(nt(a2[...], two_by_two_t(hi, lo))))

    received()
    r2[z] = added(r1, 32)
    received, sent2 = exchange(1, z_peer, z_order, lambda part: r2.at[z], r2)
    go_home(1)
    received()
    r3[y] = added(r2, Z)
    received, sent3 = exchange(2, y_peer, y_order, lambda part: r3.at[y], r3)
    go_home(2)
    received()

    square = r3[0] * r3[0]
    for q in range(1, 4):
        square = square + r3[q] * r3[q]
    old = jnp.zeros((NREL, 1), f32)
    which = lax.broadcasted_iota(jnp.int32, (NREL, 1), 0)
    for r in range(NREL):
        old = jnp.where(which == r, rel_state[r], old)
    rstate = old + jnp.sum(square, axis=1, keepdims=True) * (1.0 / D)
    scale = rel_rate / (jnp.sqrt(rstate) + epsilon)
    for q in range(4):
        lo, hi = q * ROWS, min(D, (q + 1) * ROWS)
        rel_o[:, lo:hi] = rel[:, lo:hi] - r3[q][:, : hi - lo] * scale

    for sent in (sent1, sent2, sent3):
        sent()

    @pl.loop(0, ROUNDS - 1)
    def _(k):
        for c in range(NC):
            moved_copy(k, c).wait_send()

    for c in range(NH):
        home_copy(c).wait_send()
    home_state_copy().wait_send()
    for c in range(NH):
        home_copy(c).wait_recv()
    home_state_copy().wait_recv()


def placed_back(stay_h, stay_st_h, home_h, home_st_h, rel_h, src_o, src_so, dst_o, dst_so, rel_o, *scratch):
    stay, stay_st, home, home_st, rel_v, in_sem, out_sem = scratch
    half = D // 2
    rows = [pl.ds(0, half), pl.ds(half, half)]

    def pieces(a, b, c, d, e):
        return [a.at[rows[0]], a.at[rows[1]], c.at[rows[0]], c.at[rows[1]], b, d, e]

    held = pieces(stay, stay_st, home, home_st.at[pl.ds(0, 1)], rel_v)
    came = pieces(stay_h, stay_st_h, home_h, home_st_h.at[pl.ds(0, 1)], rel_h)
    reads = [pltpu.make_async_copy(a, b, in_sem.at[i]) for i, (a, b) in enumerate(zip(came, held))]
    for copy in reads:
        copy.start()

    def writes(keep, keep_st, move, move_st):
        targets = pieces(keep, keep_st, move, move_st, rel_o)
        return [pltpu.make_async_copy(a, b, out_sem.at[i]) for i, (a, b) in enumerate(zip(held, targets))]

    core = lax.axis_index("grp") % 2

    @pl.when(core == 0)
    def _():
        for read, write in zip(reads, writes(src_o, src_so, dst_o, dst_so)):
            read.wait()
            write.start()

    @pl.when(core == 1)
    def _():
        for read, write in zip(reads, writes(dst_o, dst_so, src_o, src_so)):
            read.wait()
            write.start()

    for write in writes(src_o, src_so, dst_o, dst_so):
        write.wait()


def local(src_emb, src_state, dst_emb, dst_state, relations, rel_state, src_ids, dst_ids, rel_ids, neg_ids, lengths):
    vmem, hbm = pl.BlockSpec(memory_space=pltpu.VMEM), pl.BlockSpec(memory_space=pltpu.HBM)
    table, line = jax.ShapeDtypeStruct((D, ROWS), f32), jax.ShapeDtypeStruct((1, ROWS), f32)
    relation = jax.ShapeDtypeStruct((NREL, D), f32)
    ids = pltpu.VMEM((ROUNDS, ROWS), jnp.int32)
    results = pl.pallas_call(
        window,
        out_shape=[table, line, table, jax.ShapeDtypeStruct((8, ROWS), f32), relation],
        in_specs=[hbm] * 11,
        out_specs=[vmem] * 5,
        scratch_shapes=[
            pltpu.SMEM((ROUNDS,), jnp.int32),
            pltpu.SMEM((NREL,), f32),
            pltpu.VMEM((NREL, D), f32),
            ids,
            ids,
            ids,
            pltpu.VMEM((ROUNDS, NEG), jnp.int32),
            pltpu.VMEM((1, ROWS), f32),
            pltpu.VMEM((ROUNDS, MOVED, ROWS), f32),
            pltpu.VMEM((D, ROWS), f32),
            pltpu.VMEM((D, ROWS), f32),
            pltpu.VMEM((2 * ROWS, D), bf16),
            pltpu.VMEM((D, 2 * ROWS), bf16),
            pltpu.VMEM((D, 2 * ROWS), bf16),
            pltpu.VMEM((ROWS, 2 * ROWS), bf16),
            pltpu.VMEM((D, ROWS), f32),
            pltpu.VMEM((16, 512), f32),
            pltpu.VMEM((ROWS, ROWS), f32),
            pltpu.VMEM((ROWS, ROWS), f32),
            pltpu.VMEM((ROUNDS, 8, ROWS), jnp.int32),
            pltpu.VMEM((ROUNDS, 8, ROWS), jnp.int32),
            pltpu.VMEM((4, 8, ROWS), f32),
            pltpu.VMEM((32, 8, ROWS), f32),
            pltpu.VMEM((Z, 8, ROWS), f32),
            pltpu.VMEM((4, 8, ROWS), f32),
            pltpu.SemaphoreType.DMA((11,)),
            pltpu.SemaphoreType.DMA((ROUNDS, max(NC, NH + 1))),
            pltpu.SemaphoreType.DMA((ROUNDS, NC)),
            pltpu.SemaphoreType.DMA((NH + 1,)),
            pltpu.SemaphoreType.DMA((ROUNDS,)),
            pltpu.SemaphoreType.DMA((ROUNDS,)),
            pltpu.SemaphoreType.DMA((3, 32)),
            pltpu.SemaphoreType.DMA((3, 32)),
        ],
        compiler_params=pltpu.CompilerParams(
            collective_id=0, has_side_effects=True, vmem_limit_bytes=60 * 1024 * 1024
        ),
    )(
        lengths,
        rel_state,
        src_emb,
        src_state.reshape(1, ROWS),
        dst_emb,
        dst_state.reshape(1, ROWS),
        relations,
        src_ids,
        dst_ids,
        rel_ids,
        neg_ids,
    )
    outs = pl.pallas_call(
        placed_back,
        out_shape=[table, line, table, line, relation],
        in_specs=[hbm] * 5,
        out_specs=[hbm] * 5,
        scratch_shapes=[
            pltpu.VMEM((D, ROWS), f32),
            pltpu.VMEM((1, ROWS), f32),
            pltpu.VMEM((D, ROWS), f32),
            pltpu.VMEM((8, ROWS), f32),
            pltpu.VMEM((NREL, D), f32),
            pltpu.SemaphoreType.DMA((7,)),
            pltpu.SemaphoreType.DMA((7,)),
        ],
    )(*results)
    return (outs[0], outs[1].reshape(ROWS), outs[2], outs[3].reshape(ROWS), outs[4])


def solution(mesh):
    both = ("grp", "blk")
    placed = (
        P(None, both),
        P(both),
        P(None, both),
        P(both),
        P(),
        P(),
        P(both, None),
        P(both, None),
        P(both, None),
        P(both, None),
        P(both),
    )
    return jax.shard_map(
        local,
        mesh=mesh,
        in_specs=placed,
        out_specs=(P(None, both), P(both), P(None, both), P(both), P()),
        check_vma=False,
    )
```

```python
import jax
import jax.numpy as jnp
from jax import lax
from jax.experimental import pallas as pl
from jax.experimental.pallas import tpu as pltpu
from jax.sharding import PartitionSpec as P

learn_rate = 0.1
rel_rate = 0.5
epsilon = 1e-08

D = 400
NREL = 8
ROWS = 128
NEG = 64
ROUNDS = 8
N_GRP = 16
N_BLK = 32
Z = 16

CHUNKS = ((0, 128), (128, 128), (256, 128), (384, 16))
NC = len(CHUNKS)
HOME = ((0, 400),)
NH = len(HOME)
EARLY, MIDDLE = (0, 3), (3, 16)
STATE = D
MOVED = D + 8
MESH = pl.DeviceIdType.MESH
f32, bf16 = jnp.float32, jnp.bfloat16


def halves(x):
    hi = x.astype(bf16)
    return hi, (x - hi.astype(f32)).astype(bf16)


def nn(a, b):
    return lax.dot_general(a, b, (((1,), (0,)), ((), ())), preferred_element_type=f32)


def nt(a, b):
    return lax.dot_general(a, b, (((1,), (1,)), ((), ())), preferred_element_type=f32)


def folded(x):
    return x[:, :ROWS] + x[:, ROWS:]


def picked(table, row):
    index = jnp.broadcast_to(row, table.shape)
    return jnp.take_along_axis(table, index, axis=1, mode="promise_in_bounds")


def sub_iota():
    return lax.broadcasted_iota(jnp.int32, (ROWS, ROWS), 0)


def window(
    lengths_h,
    rel_state_h,
    src_e,
    src_s,
    dst_e,
    dst_s,
    rel_h,
    s_ids_h,
    d_ids_h,
    r_ids_h,
    n_ids_h,
    stay,
    stay_st,
    home,
    home_st,
    rel_o,
    lengths,
    rel_state,
    rel,
    s_ids,
    d_ids,
    r_ids,
    n_ids,
    line,
    mov,
    w_buf,
    s_buf,
    fixed_t,
    a2,
    d2,
    m2,
    rel_t,
    rg,
    c1,
    dv,
    packed,
    gotten,
    tiles,
    r1,
    r2,
    r3,
    in_sem,
    send_sem,
    recv_sem,
    back_sem,
    id_send,
    id_recv,
    ar_send,
    ar_recv,
):
    g, b = lax.axis_index("grp"), lax.axis_index("blk")
    y, xc, core = g // 4, (b // Z) * 4 + g % 4, g % 2
    x_hi, z = b // Z, b % Z

    def blk(by):
        return (b + by + N_BLK) % N_BLK

    ys = [(y + i) % 4 for i in range(4)]
    xcs = [(xc + i) % 8 for i in range(8)]
    xc_g, xc_b = [q % 4 for q in xcs], [(q // 4) * Z + z for q in xcs]

    def slice_peer(i):
        j, k = i // 8, i % 8
        return ys[j] * 8 + xcs[k], ys[j], (ys[j] * 4 + xc_g[k], xc_b[k])

    def z_peer(i):
        q = (z + i) % Z
        return q, q, (g, x_hi * Z + q)

    def y_peer(i):
        return ys[i], ys[i], (ys[i] * 4 + g % 4, b)

    far_y, far_x = (0, 2, 4, 2), (0, 1, 2, 3, 4, 3, 2, 1)
    slice_order = sorted(range(1, 32), key=lambda i: -(far_y[i // 8] + far_x[i % 8]))
    z_order = (8, 7, 9, 6, 10, 5, 11, 4, 12, 3, 13, 2, 14, 1, 15)
    y_order = (2, 1, 3)
    up = 1 - 2 * core

    barrier = pltpu.get_barrier_semaphore()

    def greet(device):
        pl.semaphore_signal(barrier, inc=1, device_id=device, device_id_type=MESH)

    for i in z_order:
        greet(z_peer(i)[2])
    for i in slice_order:
        greet(slice_peer(i)[2])
    greet((g, blk(-up)))
    greet((g, blk(7 * up)))
    small = [
        pltpu.make_async_copy(a, into, in_sem.at[i])
        for i, (a, into) in enumerate(
            (
                (r_ids_h, r_ids),
                (s_ids_h, s_ids),
                (rel_h, rel),
                (d_ids_h, d_ids),
                (n_ids_h, n_ids),
                (lengths_h, lengths),
                (rel_state_h, rel_state),
            )
        )
    ]
    n_small = len(small)

    def tables(keep, keep_st, move, move_st):
        return [
            pltpu.make_async_copy(a, into, in_sem.at[n_small + i])
            for i, (a, into) in enumerate(
                ((keep, stay), (keep_st, stay_st), (move, mov.at[0, pl.ds(0, D)]), (move_st, line))
            )
        ]

    @pl.when(core == 0)
    def _():
        for copy in tables(src_e, src_s, dst_e, dst_s):
            copy.start()

    @pl.when(core == 1)
    def _():
        for copy in tables(dst_e, dst_s, src_e, src_s):
            copy.start()

    for copy in small:
        copy.start()

    n_peers = len(slice_order) + len(z_order) + 2

    for copy in small:
        copy.wait()

    for k in range(ROUNDS):
        packed[k, 0:1, :] = s_ids[k : k + 1, :]
        packed[k, 1:2, :] = d_ids[k : k + 1, :]
        packed[k, 2:3, :] = r_ids[k : k + 1, :]
        packed[k, 3:4, :] = jnp.concatenate([n_ids[k : k + 1, :], jnp.full((1, ROWS - NEG), -1, jnp.int32)], axis=1)
        packed[k, 4:8, :] = jnp.full((4, ROWS), lengths[k], jnp.int32)

    wide = jnp.concatenate([rel[...], jnp.zeros((NREL, 512 - D), f32)], axis=1)
    wide = jnp.concatenate([wide, jnp.zeros((ROWS - NREL, 512), f32)], axis=0)
    rel_t[...] = wide.T[:D, :]
    for copy in tables(src_e, src_s, dst_e, dst_s):
        copy.wait()
    mov[0, STATE : STATE + 8, :] = jnp.broadcast_to(line[...], (8, ROWS))
    rg[...] = jnp.zeros_like(rg)

    def moved_copy(k, c):
        rows = pl.ds(CHUNKS[c][0], CHUNKS[c][1] + (8 if c == NC - 1 else 0))
        return pltpu.make_async_remote_copy(
            src_ref=mov.at[k, rows],
            dst_ref=mov.at[jnp.minimum(k + 1, ROUNDS - 1), rows],
            send_sem=send_sem.at[k, c],
            recv_sem=recv_sem.at[jnp.minimum(k + 1, ROUNDS - 1), c],
            device_id=(g, blk(up)),
            device_id_type=MESH,
        )

    def arrived(k, c):
        rows = pl.ds(CHUNKS[c][0], CHUNKS[c][1] + (8 if c == NC - 1 else 0))
        pltpu.make_async_remote_copy(
            src_ref=mov.at[k, rows],
            dst_ref=mov.at[k, rows],
            send_sem=send_sem.at[k, c],
            recv_sem=recv_sem.at[k, c],
            device_id=(g, blk(up)),
            device_id_type=MESH,
        ).wait_recv()

    def home_copy(c):
        rows = pl.ds(*HOME[c])
        return pltpu.make_async_remote_copy(
            src_ref=mov.at[ROUNDS - 1, rows],
            dst_ref=home.at[rows],
            send_sem=send_sem.at[ROUNDS - 1, c],
            recv_sem=back_sem.at[c],
            device_id=(g, blk(-7 * up)),
            device_id_type=MESH,
        )

    def home_state_copy():
        return pltpu.make_async_remote_copy(
            src_ref=mov.at[ROUNDS - 1, pl.ds(STATE, 8)],
            dst_ref=home_st,
            send_sem=send_sem.at[ROUNDS - 1, NH],
            recv_sem=back_sem.at[NH],
            device_id=(g, blk(-7 * up)),
            device_id_type=MESH,
        )

    def stepped(k, grad):
        state = mov[k, STATE : STATE + 8, :] + jnp.sum(grad * grad, axis=0, keepdims=True) * (1.0 / D)
        scale = (learn_rate / (jnp.sqrt(state) + epsilon))[0:1]
        mov[k, STATE : STATE + 8, :] = state
        for c, (r0, n) in enumerate(CHUNKS):
            mov[k, r0 : r0 + n, :] = mov[k, r0 : r0 + n, :] - grad[r0 : r0 + n] * scale
            if not isinstance(k, int):
                moved_copy(k, c).start()

    def settled(grad):
        new = stay_st[...] + jnp.sum(grad * grad, axis=0, keepdims=True) * (1.0 / D)
        stay_st[...] = new
        stay[...] = stay[...] - grad * (learn_rate / (jnp.sqrt(new) + epsilon))

    def related(h, tile):
        hot = (lax.broadcasted_iota(jnp.int32, (16, ROWS), 0) == tile[2:3]).astype(f32).astype(bf16)
        rg[:, :D] = rg[:, :D] + nt(jnp.concatenate([hot, hot], axis=1), both(s_buf[...] * h))

    def coefficients(tile):
        rows = sub_iota()
        valid = (lax.broadcasted_iota(jnp.int32, (1, ROWS), 1) < tile[4:5]).astype(f32)
        hit = (rows == tile[1:2]).astype(f32)
        count = jnp.sum((rows == tile[3:4]).astype(f32), axis=1, keepdims=True)
        return (count + hit) * valid, hit * valid

    def one_hot2(row):
        hot = (sub_iota() == row).astype(f32).astype(bf16)
        return jnp.concatenate([hot, hot], axis=1)

    def quadrants(x):
        return (x[:ROWS, :ROWS] + x[ROWS:, ROWS:]) + (x[:ROWS, ROWS:] + x[ROWS:, :ROWS])

    def two_by_two(hi, lo):
        line = jnp.concatenate([hi, lo], axis=1)
        return jnp.concatenate([line, line], axis=0)

    def two_by_two_t(hi, lo):
        return jnp.concatenate([jnp.concatenate([hi, hi], axis=1), jnp.concatenate([lo, lo], axis=1)], axis=0)

    def split_into(ref, r0, n, x):
        hi, lo = halves(x)
        ref[r0 : r0 + n, :ROWS] = hi
        ref[r0 : r0 + n, ROWS:] = lo

    def transposed_into(x):
        hi, lo = halves(x.T)
        fixed_t[:ROWS, :] = hi
        fixed_t[ROWS:, :] = lo

    def left_over(hi, lo, h):
        m2[:, :ROWS] = hi
        m2[:, ROWS:] = lo
        w_buf[...] = w_buf[...] * h

    def both(x):
        return jnp.concatenate(halves(x), axis=1)

    @pl.when(core == 0)
    def _():
        def prepare(k):
            tile = packed[k]
            w = picked(rel_t[...], tile[2:3])
            s = picked(stay[...], tile[0:1])
            a = s * w
            w_buf[...] = w
            s_buf[...] = s
            split_into(a2, 0, D, a)
            transposed_into(a)
            c, v = coefficients(tile)
            c1[...] = c.T
            dv[...] = v.T

        prepare(0)
        pl.semaphore_wait(barrier, n_peers)

        @pl.loop(0, ROUNDS)
        def _(k):
            total = jnp.zeros((2 * ROWS, 2 * ROWS), f32)
            for c, (r0, n) in enumerate(CHUNKS):

                @pl.when(k > 0)
                def _():
                    arrived(k, c)

                split_into(d2, r0, n, mov[k, r0 : r0 + n, :])
                total = total + nn(fixed_t[:, r0 : r0 + n], d2[r0 : r0 + n, :])
            m = c1[...] * jax.nn.sigmoid(quadrants(total)) - dv[...]
            hi, lo = halves(m)

            @pl.when(k < ROUNDS - 1)
            def _():
                stepped(k, folded(nn(a2[...], two_by_two(hi, lo))))

            h = folded(nt(d2[...], two_by_two_t(hi, lo)))
            tile = packed[k]
            related(h, tile)

            @pl.when(k < ROUNDS - 1)
            def _():
                settled(nt(both(w_buf[...] * h), one_hot2(tile[0:1])))
                prepare(k + 1)

            @pl.when(k == ROUNDS - 1)
            def _():
                left_over(hi, lo, h)

    @pl.when(core == 1)
    def _():
        for k in range(2, ROUNDS):
            greet((g, blk(k)))
        gotten[0] = packed[0]

        def id_copy(k):
            return pltpu.make_async_remote_copy(
                src_ref=packed.at[k],
                dst_ref=gotten.at[k],
                send_sem=id_send.at[k],
                recv_sem=id_recv.at[k],
                device_id=(g, blk(-k)),
                device_id_type=MESH,
            )

        def prepare(k):
            tile = gotten[k]
            w_buf[...] = picked(rel_t[...], tile[2:3])
            d = stay[...]
            split_into(d2, 0, D, d)
            transposed_into(d)
            c, v = coefficients(tile)
            c1[...] = c
            dv[...] = v

        prepare(0)
        pl.semaphore_wait(barrier, n_peers + ROUNDS - 2)
        for k in range(1, ROUNDS):
            id_copy(k).start()

        @pl.loop(0, ROUNDS)
        def _(k):
            tile = gotten[k]
            total = jnp.zeros((2 * ROWS, 2 * ROWS), f32)
            for c, (r0, n) in enumerate(CHUNKS):

                @pl.when(k > 0)
                def _():
                    arrived(k, c)

                s = picked(mov[k, r0 : r0 + n, :], tile[0:1])
                s_buf[r0 : r0 + n, :] = s
                split_into(a2, r0, n, s * w_buf[r0 : r0 + n, :])
                total = total + nn(fixed_t[:, r0 : r0 + n], a2[r0 : r0 + n, :])
            m = c1[...] * jax.nn.sigmoid(quadrants(total)) - dv[...]
            hi, lo = halves(m)
            h = folded(nn(d2[...], two_by_two(hi, lo)))

            @pl.when(k < ROUNDS - 1)
            def _():
                stepped(k, nt(both(w_buf[...] * h), one_hot2(tile[0:1])))

            related(h, tile)

            @pl.when(k < ROUNDS - 1)
            def _():
                settled(folded(nt(a2[...], two_by_two_t(hi, lo))))
                id_copy(k + 1).wait_recv()
                prepare(k + 1)

            @pl.when(k == ROUNDS - 1)
            def _():
                left_over(hi, lo, h)

        for k in range(1, ROUNDS):
            id_copy(k).wait_send()

    for q in range(4):
        tiles[q] = rg[:NREL, q * ROWS : (q + 1) * ROWS]

    def exchange(stage, peer, order, source, buf):
        def copy(i, slot):
            _, part, device = peer(i)
            return pltpu.make_async_remote_copy(
                src_ref=source(part),
                dst_ref=buf.at[slot],
                send_sem=ar_send.at[stage, i],
                recv_sem=ar_recv.at[stage, slot],
                device_id=device,
                device_id_type=MESH,
            )

        mine = peer(0)[0]
        for i in order:
            copy(i, mine).start()

        def wait_recv():
            for i in order:
                copy(i, peer(i)[0]).wait_recv()

        def wait_send():
            for i in order:
                copy(i, mine).wait_send()

        return wait_recv, wait_send

    home_z = (z + Z - 7 * up) % Z

    def go_home(turn):
        early = (home_z >= EARLY[0]) & (home_z < EARLY[1])
        middle = (home_z >= MIDDLE[0]) & (home_z < MIDDLE[1])
        now = (early, middle, jnp.logical_not(early | middle))[turn]

        @pl.when(now)
        def _():
            home_state_copy().start()
            for c in range(NH):
                home_copy(c).start()

    def added(buf, n):
        value = buf[0]
        for q in range(1, n):
            value = value + buf[q]
        return value

    r1[y * 8 + xc] = tiles[y]
    received, sent1 = exchange(0, slice_peer, slice_order, lambda part: tiles.at[part], r1)

    hi, lo = m2[:, :ROWS], m2[:, ROWS:]
    last = ROUNDS - 1

    @pl.when(core == 0)
    def _():
        stepped(last, folded(nn(a2[...], two_by_two(hi, lo))))

    @pl.when(core == 1)
    def _():
        stepped(last, nt(both(w_buf[...]), one_hot2(gotten[last, 0:1])))

    go_home(0)

    @pl.when(core == 0)
    def _():
        settled(nt(both(w_buf[...]), one_hot2(packed[last, 0:1])))

    @pl.when(core == 1)
    def _():
        settled(folded(nt(a2[...], two_by_two_t(hi, lo))))

    received()
    r2[z] = added(r1, 32)
    received, sent2 = exchange(1, z_peer, z_order, lambda part: r2.at[z], r2)
    go_home(1)
    received()
    r3[y] = added(r2, Z)
    received, sent3 = exchange(2, y_peer, y_order, lambda part: r3.at[y], r3)
    go_home(2)
    received()

    square = r3[0] * r3[0]
    for q in range(1, 4):
        square = square + r3[q] * r3[q]
    old = jnp.zeros((NREL, 1), f32)
    which = lax.broadcasted_iota(jnp.int32, (NREL, 1), 0)
    for r in range(NREL):
        old = jnp.where(which == r, rel_state[r], old)
    rstate = old + jnp.sum(square, axis=1, keepdims=True) * (1.0 / D)
    scale = rel_rate / (jnp.sqrt(rstate) + epsilon)
    for q in range(4):
        lo, hi = q * ROWS, min(D, (q + 1) * ROWS)
        rel_o[:, lo:hi] = rel[:, lo:hi] - r3[q][:, : hi - lo] * scale

    for sent in (sent1, sent2, sent3):
        sent()

    @pl.loop(0, ROUNDS - 1)
    def _(k):
        for c in range(NC):
            moved_copy(k, c).wait_send()

    for c in range(NH):
        home_copy(c).wait_send()
    home_state_copy().wait_send()
    for c in range(NH):
        home_copy(c).wait_recv()
    home_state_copy().wait_recv()


def placed_back(stay_h, stay_st_h, home_h, home_st_h, rel_h, src_o, src_so, dst_o, dst_so, rel_o, *scratch):
    stay, stay_st, home, home_st, rel_v, in_sem, out_sem = scratch
    half = D // 2
    rows = [pl.ds(0, half), pl.ds(half, half)]

    def pieces(a, b, c, d, e):
        return [a.at[rows[0]], a.at[rows[1]], c.at[rows[0]], c.at[rows[1]], b, d, e]

    held = pieces(stay, stay_st, home, home_st.at[pl.ds(0, 1)], rel_v)
    came = pieces(stay_h, stay_st_h, home_h, home_st_h.at[pl.ds(0, 1)], rel_h)
    reads = [pltpu.make_async_copy(a, b, in_sem.at[i]) for i, (a, b) in enumerate(zip(came, held))]
    for copy in reads:
        copy.start()

    def writes(keep, keep_st, move, move_st):
        targets = pieces(keep, keep_st, move, move_st, rel_o)
        return [pltpu.make_async_copy(a, b, out_sem.at[i]) for i, (a, b) in enumerate(zip(held, targets))]

    core = lax.axis_index("grp") % 2

    @pl.when(core == 0)
    def _():
        for read, write in zip(reads, writes(src_o, src_so, dst_o, dst_so)):
            read.wait()
            write.start()

    @pl.when(core == 1)
    def _():
        for read, write in zip(reads, writes(dst_o, dst_so, src_o, src_so)):
            read.wait()
            write.start()

    for write in writes(src_o, src_so, dst_o, dst_so):
        write.wait()


def local(src_emb, src_state, dst_emb, dst_state, relations, rel_state, src_ids, dst_ids, rel_ids, neg_ids, lengths):
    vmem, hbm = pl.BlockSpec(memory_space=pltpu.VMEM), pl.BlockSpec(memory_space=pltpu.HBM)
    table, line = jax.ShapeDtypeStruct((D, ROWS), f32), jax.ShapeDtypeStruct((1, ROWS), f32)
    relation = jax.ShapeDtypeStruct((NREL, D), f32)
    ids = pltpu.VMEM((ROUNDS, ROWS), jnp.int32)
    results = pl.pallas_call(
        window,
        out_shape=[table, line, table, jax.ShapeDtypeStruct((8, ROWS), f32), relation],
        in_specs=[hbm] * 11,
        out_specs=[vmem] * 5,
        scratch_shapes=[
            pltpu.SMEM((ROUNDS,), jnp.int32),
            pltpu.SMEM((NREL,), f32),
            pltpu.VMEM((NREL, D), f32),
            ids,
            ids,
            ids,
            pltpu.VMEM((ROUNDS, NEG), jnp.int32),
            pltpu.VMEM((1, ROWS), f32),
            pltpu.VMEM((ROUNDS, MOVED, ROWS), f32),
            pltpu.VMEM((D, ROWS), f32),
            pltpu.VMEM((D, ROWS), f32),
            pltpu.VMEM((2 * ROWS, D), bf16),
            pltpu.VMEM((D, 2 * ROWS), bf16),
            pltpu.VMEM((D, 2 * ROWS), bf16),
            pltpu.VMEM((ROWS, 2 * ROWS), bf16),
            pltpu.VMEM((D, ROWS), f32),
            pltpu.VMEM((16, 512), f32),
            pltpu.VMEM((ROWS, ROWS), f32),
            pltpu.VMEM((ROWS, ROWS), f32),
            pltpu.VMEM((ROUNDS, 8, ROWS), jnp.int32),
            pltpu.VMEM((ROUNDS, 8, ROWS), jnp.int32),
            pltpu.VMEM((4, 8, ROWS), f32),
            pltpu.VMEM((32, 8, ROWS), f32),
            pltpu.VMEM((Z, 8, ROWS), f32),
            pltpu.VMEM((4, 8, ROWS), f32),
            pltpu.SemaphoreType.DMA((11,)),
            pltpu.SemaphoreType.DMA((ROUNDS, max(NC, NH + 1))),
            pltpu.SemaphoreType.DMA((ROUNDS, NC)),
            pltpu.SemaphoreType.DMA((NH + 1,)),
            pltpu.SemaphoreType.DMA((ROUNDS,)),
            pltpu.SemaphoreType.DMA((ROUNDS,)),
            pltpu.SemaphoreType.DMA((3, 32)),
            pltpu.SemaphoreType.DMA((3, 32)),
        ],
        compiler_params=pltpu.CompilerParams(
            collective_id=0, has_side_effects=True, vmem_limit_bytes=60 * 1024 * 1024
        ),
    )(
        lengths,
        rel_state,
        src_emb,
        src_state.reshape(1, ROWS),
        dst_emb,
        dst_state.reshape(1, ROWS),
        relations,
        src_ids,
        dst_ids,
        rel_ids,
        neg_ids,
    )
    outs = pl.pallas_call(
        placed_back,
        out_shape=[table, line, table, line, relation],
        in_specs=[hbm] * 5,
        out_specs=[hbm] * 5,
        scratch_shapes=[
            pltpu.VMEM((D, ROWS), f32),
            pltpu.VMEM((1, ROWS), f32),
            pltpu.VMEM((D, ROWS), f32),
            pltpu.VMEM((8, ROWS), f32),
            pltpu.VMEM((NREL, D), f32),
            pltpu.SemaphoreType.DMA((7,)),
            pltpu.SemaphoreType.DMA((7,)),
        ],
    )(*results)
    return (outs[0], outs[1].reshape(ROWS), outs[2], outs[3].reshape(ROWS), outs[4])


def solution(mesh):
    both = ("grp", "blk")
    placed = (
        P(None, both),
        P(both),
        P(None, both),
        P(both),
        P(),
        P(),
        P(both, None),
        P(both, None),
        P(both, None),
        P(both, None),
        P(both),
    )
    return jax.shard_map(
        local,
        mesh=mesh,
        in_specs=placed,
        out_specs=(P(None, both), P(both), P(None, both), P(both), P()),
        check_vma=False,
    )
```
